512 devices in a mesh: ens: 16 (over y_lo, x, core), lat: 16 (over z), dp: 2 (over y_hi).
Axes of the slice: x: 4, y: 4 (y_hi: 2, y_lo: 2; y = y_hi * 2 + y_lo), z: 16, core: 2. Of those that a mesh axis runs over, the one named last changes fastest.
Arguments:
- features: bfloat16 [2, 16, 256, 32, 512], P('dp', 'ens', None, 'lat'), may hold values from -6 to 6
- members_out: bfloat16 [2, 16, 72, 32, 512], P('dp', 'ens', None, 'lat'), may hold values from -6 to 6
- observed: float32 [2, 72, 32, 512], P('dp', None, 'lat'), may hold values from -6 to 6
- conv_weight: bfloat16 [9, 72, 256], replicated, may hold values from -0.125 to 0.125
- lat_weight: float32 [32], P('lat'), may hold values from 0.2 to 1
- var_weight: float32 [72], replicated, may hold values from 0.3 to 3
- land_mask: int32 [32, 512], P('lat'), may hold values 0 or 1
Outputs:
- feature_grads: bfloat16 [2, 16, 256, 32, 512], P('dp', 'ens', None, 'lat')
- grad_weight: float32 [9, 72, 256], replicated
The draws below stay inside these ranges and needn't reach their ends.
All inputs are finite; a program needn't handle non-finite values. No bound on the sum of `land_mask` on one device may be relied on, other than what follows from the above.
Results may differ from the reference program's by a relative error of at most 0.0049.
Values may be sent and summed in bfloat16 or wider, within the bound.
A program may use at most 64 MiB of HBM per device.

```python
import math
import jax
import jax.numpy as jnp
from jax import lax

CHANNELS = 256
VARIABLES = 72
LONS = 512
MEMBERS = 16
SAMPLES = 2
NLAT = 32


def set_ends(result, key, smallest, top_value):
    place = [jax.random.randint(jax.random.fold_in(key, axis), (), 0, length) for axis, length in enumerate(result.shape)]
    longest = result.shape.index(max(result.shape))
    next_to = place[:longest] + [(place[longest] + 1) % result.shape[longest]] + place[longest + 1:]
    return result.at[tuple(place)].set(smallest).at[tuple(next_to)].set(top_value)


def shard_levels(key, shape, pieces, least, top_value):
    gain = 1.0
    for position, shards_of in pieces:
        draws = jax.random.uniform(jax.random.fold_in(jax.random.fold_in(key, 6), position), (shards_of,), jnp.float32, least / len(pieces), top_value / len(pieces))
        gain = gain * jnp.repeat(jnp.exp(draws), shape[position] // shards_of).reshape((-1,) + (1,) * (len(shape) - 1 - position))
    return gain


def bell_draw(rng, shape, spread, most, shards=(), dtype=jnp.bfloat16):
    values = spread * jax.random.normal(rng, shape, jnp.float32)
    if shards:
        values = values * shard_levels(rng, shape, shards, -0.22, 0.18)
    return jnp.clip(values, -most, most).astype(dtype)


def setup_inputs(seed: int = 0) -> dict:
    keys = jax.random.split(jax.random.key(seed), 8)
    return {
        "features": bell_draw(keys[0], (SAMPLES, MEMBERS, CHANNELS, NLAT, LONS), 1.0, 6.0, ((0, 2), (1, 16), (3, 16))),
        "members_out": bell_draw(keys[1], (SAMPLES, MEMBERS, VARIABLES, NLAT, LONS), 1.0, 6.0, ((0, 2), (1, 16), (3, 16))),
        "observed": bell_draw(keys[2], (SAMPLES, VARIABLES, NLAT, LONS), 1.0, 6.0, ((0, 2), (2, 16)), jnp.float32),
        "conv_weight": bell_draw(keys[3], (9, VARIABLES, CHANNELS), (9 * CHANNELS) ** -0.5, 0.125),
        "lat_weight": jnp.clip(jnp.exp(math.log(1.0) - 1.609438 * jax.random.uniform(keys[4], (NLAT,), jnp.float32) ** shard_levels(keys[4], (NLAT,), ((0, 16),), -0.2, 0.2)), 0.2, 1.0),
        "var_weight": jnp.clip(jnp.exp(jax.random.uniform(keys[5], (VARIABLES,), jnp.float32, math.log(0.3), math.log(3.0))), 0.3, 3.0),
        "land_mask": set_ends((jax.random.randint(keys[6], (NLAT, LONS), 0, 3) < 1).astype(jnp.int32), jax.random.fold_in(keys[6], 1), 0, 1),
    }


def tap_stack(member_grads, lat_rows, lon_cells):
    padded = jnp.pad(member_grads, ((0, 0), (1, 1), (1, 1)))
    slices = []
    for row_shift in (-1, 0, 1):
        for col_shift in (-1, 0, 1):
            slices.append(padded[:, 1 - row_shift:1 - row_shift + lat_rows, 1 - col_shift:1 - col_shift + lon_cells])
    return jnp.stack(slices).reshape(9 * member_grads.shape[0], lat_rows * lon_cells)

def score_grads(members_out, observed, lat_weight, var_weight, land_mask):
    fields = members_out.astype(jnp.float32)
    member_count = fields.shape[1]

    def add_member(member_index, running):
        another = lax.dynamic_index_in_dim(fields, member_index, 1, keepdims=True)
        return running + jnp.sign(fields - another)
    pair_sums = lax.fori_loop(0, member_count, add_member, jnp.zeros_like(fields))
    cell_weight = lat_weight[None, :, None] * var_weight[:, None, None] * (1.0 + land_mask.astype(jnp.float32))[None]
    out_grads = cell_weight[None, None] * (jnp.sign(fields - observed[:, None]) - pair_sums / (member_count - 1))
    return out_grads.astype(jnp.bfloat16)

def reference(features, members_out, observed, conv_weight, lat_weight, var_weight, land_mask):
    out_grads = score_grads(members_out, observed, lat_weight, var_weight, land_mask)
    samples, members, channels, lat_rows, lon_cells = features.shape
    variables = members_out.shape[2]
    flat_feats = features.reshape(samples * members, channels, lat_rows, lon_cells)
    flat_grads = out_grads.reshape(samples * members, variables, lat_rows, lon_cells)
    flat_weight = conv_weight.astype(jnp.float32).reshape(9 * variables, channels)

    def per_member(summed, member_pair):
        member_feats, member_grads = member_pair
        tap_rows = tap_stack(member_grads.astype(jnp.float32), lat_rows, lon_cells)
        feature_grad = jnp.dot(flat_weight.T, tap_rows, preferred_element_type=jnp.float32)
        plain_feats = member_feats.astype(jnp.float32).reshape(channels, lat_rows * lon_cells)
        weight_grad = jnp.dot(tap_rows, plain_feats.T, preferred_element_type=jnp.float32)
        return (summed + weight_grad, feature_grad.astype(jnp.bfloat16))
    summed, feature_grads = lax.scan(per_member, jnp.zeros((9 * variables, channels), jnp.float32), (flat_feats, flat_grads))
    scale = 1.0 / math.sqrt(samples * members * lat_rows * lon_cells)
    feature_grads = feature_grads.reshape(samples, members, channels, lat_rows, lon_cells)
    return (feature_grads, (summed * scale).reshape(9, variables, channels))
```

```python
import functools
import math

import jax
import jax.numpy as jnp
from jax import lax
from jax.experimental import pallas as pl
from jax.experimental.pallas import tpu as pltpu
from jax.sharding import PartitionSpec as P

MESH = pl.DeviceIdType.MESH
BF16 = jnp.bfloat16
F32 = jnp.float32

MEMBERS = 16
BANDS = 16
VARS = 72
PAD_VARS = 80
LONS = 512
CHANS = 256
OWNERS = 12
CHUNK = 48
RAW = VARS * 8
TAPS = 9 * PAD_VARS
CHIPS = 16
PIECE = 48
ROWS = CHIPS * PIECE


def kernel(
    members_ref, obs_ref, feats_ref, weight_ref, lat_ref, var_ref, land_ref,
    fg_ref, gw_ref,
    mbuf, obuf, gbuf, gf, obs, feats, weight, stack, fgbuf, wg, wgin, pieces, rs, za, zb,
    exch_send, exch_recv, back_send, back_recv, halo_send, halo_recv, core_send, core_recv,
    rs_send, rs_recv, za_send, za_recv, zb_send, zb_recv, ag_send, ag_recv, fwd_send, fwd_recv,
    load_sem, store_sem,
):
    ens = lax.axis_index("ens")
    lat = lax.axis_index("lat")
    dp = lax.axis_index("dp")
    core = lax.rem(ens, 2)
    chip = dp * 8 + ens // 2
    up = lax.rem(lat + 1, BANDS)
    down = lax.rem(lat + BANDS - 1, BANDS)
    zlo = lax.rem(lat, 4)
    zhi = lat // 4

    def at(e, l, d):
        return (e, l, d)

    barrier = pltpu.get_barrier_semaphore()

    def greet(e, l, d):
        pl.semaphore_signal(barrier, inc=1, device_id=at(e, l, d), device_id_type=MESH)

    def greet_ens(k, c):
        greet(lax.rem(ens + k, MEMBERS), lat, dp)
        return c

    lax.fori_loop(1, MEMBERS, greet_ens, 0)

    def greet_dp(k, c):
        greet(2 * k + core, lat, 1 - dp)
        return c

    lax.fori_loop(0, 8, greet_dp, 0)
    greet(ens, up, dp)
    greet(ens, down, dp)

    def greet_z(k, c):
        greet(ens, zhi * 4 + lax.rem(zlo + k, 4), dp)
        greet(ens, lax.rem(lat + 4 * k, BANDS), dp)
        return c

    lax.fori_loop(1, 4, greet_z, 0)

    load_obs = pltpu.make_async_copy(obs_ref.at[pl.ds(jnp.minimum(ens, OWNERS - 1) * CHUNK, CHUNK)], obs, load_sem.at[0])
    load_obs.start()
    load_feats = pltpu.make_async_copy(feats_ref, feats, load_sem.at[1])
    load_feats.start()
    load_weight = pltpu.make_async_copy(weight_ref, weight, load_sem.at[2])
    load_weight.start()

    pl.semaphore_wait(barrier, 15 + 8 + 2 + 6)

    def send_chunk(k, c):
        owner = lax.rem(ens + k, MEMBERS)

        @pl.when(owner < OWNERS)
        def _():
            pltpu.make_async_remote_copy(
                src_ref=members_ref.at[pl.ds(owner * CHUNK, CHUNK)],
                dst_ref=mbuf.at[ens],
                send_sem=exch_send, recv_sem=exch_recv,
                device_id=at(owner, lat, dp), device_id_type=MESH,
            ).start()
        return c

    lax.fori_loop(1, MEMBERS, send_chunk, 0)
    owned = ens < OWNERS

    @pl.when(owned)
    def _():
        mine = pltpu.make_async_copy(members_ref.at[pl.ds(ens * CHUNK, CHUNK)], mbuf.at[ens], exch_recv)
        mine.start()
    load_obs.wait()

    @pl.when(owned)
    def _():
        pltpu.make_async_copy(mbuf, mbuf, exch_recv).wait()

        one = jnp.ones((16, 128), F32)
        zero = jnp.zeros((16, 128), F32)
        row = lax.broadcasted_iota(jnp.int32, (8, 128), 0)
        lat_rows = jnp.where(lax.rem(row, 2) == 0, lat_ref[0], lat_ref[1])
        land_rows = 1.0 + land_ref[...].astype(F32)

        def tile(u, c):
            rows = pl.ds(pl.multiple_of(u * 16, 16), 16)
            vals = [mbuf[m, rows, :].astype(F32) for m in range(MEMBERS)]
            sums = [None] * MEMBERS
            for i in range(MEMBERS):
                for j in range(i + 1, MEMBERS):
                    s = jnp.where(vals[i] > vals[j], one, jnp.where(vals[i] < vals[j], -one, zero))
                    sums[i] = s if sums[i] is None else sums[i] + s
                    sums[j] = -s if sums[j] is None else sums[j] - s
            seen = obs[rows, :]
            v0 = ens * 6 + u * 2
            cell = jnp.concatenate(
                [(lat_rows * var_ref[v0]) * land_rows, (lat_rows * var_ref[v0 + 1]) * land_rows], axis=0
            )
            for m in range(MEMBERS):
                s = jnp.where(vals[m] > seen, one, jnp.where(vals[m] < seen, -one, zero))
                obuf[m, rows, :] = (cell * (s - sums[m] / (MEMBERS - 1))).astype(BF16)
            return c

        lax.fori_loop(0, CHUNK // 16, tile, 0)

        def send_back(k, c):
            m = lax.rem(ens + k, MEMBERS)
            pltpu.make_async_remote_copy(
                src_ref=obuf.at[m],
                dst_ref=gbuf.at[pl.ds(ens * CHUNK, CHUNK)],
                send_sem=back_send, recv_sem=back_recv,
                device_id=at(m, lat, dp), device_id_type=MESH,
            ).start()
            return c

        lax.fori_loop(1, MEMBERS, send_back, 0)
        pltpu.make_async_copy(obuf.at[ens], gbuf.at[pl.ds(ens * CHUNK, CHUNK)], back_recv).start()

    pltpu.make_async_copy(gbuf, gbuf, back_recv).wait()

    col = lax.broadcasted_iota(jnp.int32, (PAD_VARS, LONS), 1)

    def put(slot, x):
        stack[slot, 1] = x.astype(BF16)
        stack[slot, 0] = jnp.where(col == 0, 0.0, pltpu.roll(x, 1, 1)).astype(BF16)
        stack[slot, 2] = jnp.where(col == LONS - 1, 0.0, pltpu.roll(x, LONS - 1, 1)).astype(BF16)

    gf[...] = gbuf[...].astype(F32)
    rows = []
    for r in range(2):
        x = jnp.concatenate([gf[pl.ds(2 * l + r, VARS, stride=8), :] for l in range(4)], axis=1)
        rows.append(jnp.concatenate([x, jnp.zeros((PAD_VARS - VARS, LONS), F32)], axis=0))
        stack[r + 1, 1] = rows[r].astype(BF16)
    halo = []
    for r in range(2):
        halo.append(pltpu.make_async_remote_copy(
            src_ref=stack.at[r + 1, 1], dst_ref=stack.at[3 - 3 * r, 1],
            send_sem=halo_send.at[r], recv_sem=halo_recv.at[r],
            device_id=at(ens, down if r == 0 else up, dp), device_id_type=MESH,
        ))
        halo[r].start()
    for r in range(2):
        stack[r + 1, 0] = jnp.where(col == 0, 0.0, pltpu.roll(rows[r], 1, 1)).astype(BF16)
        stack[r + 1, 2] = jnp.where(col == LONS - 1, 0.0, pltpu.roll(rows[r], LONS - 1, 1)).astype(BF16)
    load_feats.wait()
    load_weight.wait()
    for r in range(2):
        halo[r].wait()
    put(3, jnp.where(lat == BANDS - 1, 0.0, stack[3, 1].astype(F32)))
    put(0, jnp.where(lat == 0, 0.0, stack[0, 1].astype(F32)))

    def half(h):
        total = None
        for r in range(2):
            taps = stack[pl.ds(r, 3)].reshape(TAPS, LONS)
            part = lax.dot_general(
                taps, feats[r, pl.ds(pl.multiple_of(h * 128, 128), 128), :], (((1,), (1,)), ((), ())),
                preferred_element_type=F32,
            )
            total = part if total is None else total + part
        return total

    wg[0] = half(1 - core)
    to_core = pltpu.make_async_remote_copy(
        src_ref=wg.at[0], dst_ref=wgin, send_sem=core_send, recv_sem=core_recv,
        device_id=at(ens + 1 - 2 * core, lat, dp), device_id_type=MESH,
    )
    to_core.start()
    wg[1] = half(core)
    to_core.wait()
    summed = wg[1] + wgin[...]
    pieces[pl.ds(0, TAPS), :] = summed.astype(BF16)
    pieces[pl.ds(TAPS, ROWS - TAPS), :] = jnp.zeros((ROWS - TAPS, 128), BF16)

    def send_piece(k, c):
        q = lax.rem(chip + k, CHIPS)
        pltpu.make_async_remote_copy(
            src_ref=pieces.at[pl.ds(q * PIECE, PIECE)], dst_ref=rs.at[chip],
            send_sem=rs_send, recv_sem=rs_recv,
            device_id=at(lax.rem(q, 8) * 2 + core, lat, q // 8), device_id_type=MESH,
        ).start()
        return c

    lax.fori_loop(1, CHIPS, send_piece, 0)
    pltpu.make_async_copy(pieces.at[pl.ds(chip * PIECE, PIECE)], rs.at[chip], rs_recv).start()

    for r in range(2):
        taps = stack[pl.ds(r, 3)].reshape(TAPS, LONS)
        fgbuf[r] = jnp.dot(weight[...], taps, preferred_element_type=F32).astype(BF16)
    store_fg = pltpu.make_async_copy(fgbuf, fg_ref, store_sem)
    store_fg.start()

    pltpu.make_async_copy(rs, rs, rs_recv).wait()
    piece = rs[0].astype(F32)
    for q in range(1, CHIPS):
        piece = piece + rs[q].astype(F32)

    za[zlo] = piece.astype(BF16)
    for k in range(1, 4):
        pltpu.make_async_remote_copy(
            src_ref=za.at[zlo], dst_ref=za.at[zlo], send_sem=za_send, recv_sem=za_recv,
            device_id=at(ens, zhi * 4 + lax.rem(zlo + k, 4), dp), device_id_type=MESH,
        ).start()
    pltpu.make_async_copy(za.at[pl.ds(0, 3)], za.at[pl.ds(0, 3)], za_recv).wait()
    piece = (za[0].astype(F32) + za[1].astype(F32)) + (za[2].astype(F32) + za[3].astype(F32))
    zb[zhi] = piece.astype(BF16)
    for k in range(1, 4):
        pltpu.make_async_remote_copy(
            src_ref=zb.at[zhi], dst_ref=zb.at[zhi], send_sem=zb_send, recv_sem=zb_recv,
            device_id=at(ens, lax.rem(lat + 4 * k, BANDS), dp), device_id_type=MESH,
        ).start()
    pltpu.make_async_copy(zb.at[pl.ds(0, 3)], zb.at[pl.ds(0, 3)], zb_recv).wait()
    piece = (zb[0].astype(F32) + zb[1].astype(F32)) + (zb[2].astype(F32) + zb[3].astype(F32))
    za[4] = piece.astype(BF16)

    def send_sum(k, c):
        q = lax.rem(chip + k, CHIPS)
        pltpu.make_async_remote_copy(
            src_ref=za.at[4], dst_ref=gw_ref.at[core, chip],
            send_sem=ag_send, recv_sem=ag_recv,
            device_id=at(lax.rem(q, 8) * 2 + core, lat, q // 8), device_id_type=MESH,
        ).start()
        return c

    lax.fori_loop(1, CHIPS, send_sum, 0)
    pltpu.make_async_copy(za.at[4], gw_ref.at[core, chip], ag_recv).start()
    pltpu.make_async_copy(rs, rs, ag_recv).wait()
    forward = pltpu.make_async_remote_copy(
        src_ref=gw_ref.at[core], dst_ref=gw_ref.at[core], send_sem=fwd_send, recv_sem=fwd_recv,
        device_id=at(ens + 1 - 2 * core, lat, dp), device_id_type=MESH,
    )
    forward.start()

    @pl.when(owned)
    def _():
        pltpu.make_async_copy(mbuf.at[pl.ds(0, OWNERS - 1)], mbuf.at[pl.ds(0, OWNERS - 1)], exch_send).wait()
        pltpu.make_async_copy(obuf.at[pl.ds(0, MEMBERS - 1)], obuf.at[pl.ds(0, MEMBERS - 1)], back_send).wait()

    @pl.when(jnp.logical_not(owned))
    def _():
        pltpu.make_async_copy(mbuf.at[pl.ds(0, OWNERS)], mbuf.at[pl.ds(0, OWNERS)], exch_send).wait()

    pltpu.make_async_copy(rs.at[pl.ds(0, CHIPS - 1)], rs.at[pl.ds(0, CHIPS - 1)], rs_send).wait()
    pltpu.make_async_copy(za.at[pl.ds(0, 3)], za.at[pl.ds(0, 3)], za_send).wait()
    pltpu.make_async_copy(zb.at[pl.ds(0, 3)], zb.at[pl.ds(0, 3)], zb_send).wait()
    pltpu.make_async_copy(rs.at[pl.ds(0, CHIPS - 1)], rs.at[pl.ds(0, CHIPS - 1)], ag_send).wait()
    store_fg.wait()
    forward.wait()


def raw_rows(x):
    lead = x.shape[0]
    return x.reshape(lead, 2, 4, 128).transpose(0, 2, 1, 3).reshape(lead * 8, 128)


def local(features, members_out, observed, conv_weight, lat_weight, var_weight, land_mask):
    members = raw_rows(members_out[0, 0])
    obs = raw_rows(observed[0])
    land = raw_rows(land_mask[None])
    feats = features[0, 0].transpose(1, 0, 2)
    weight = jnp.pad(conv_weight[::-1], ((0, 0), (0, PAD_VARS - VARS), (0, 0))).reshape(TAPS, CHANS).T
    any_spec = pl.BlockSpec(memory_space=pl.ANY)
    vmem_spec = pl.BlockSpec(memory_space=pltpu.VMEM)
    smem_spec = pl.BlockSpec(memory_space=pltpu.SMEM)
    dma = pltpu.SemaphoreType.DMA
    fg, gw = pl.pallas_call(
        kernel,
        out_shape=(
            jax.ShapeDtypeStruct((2, CHANS, LONS), BF16),
            jax.ShapeDtypeStruct((2, CHIPS, PIECE, 128), BF16),
        ),
        in_specs=[any_spec, any_spec, any_spec, any_spec, smem_spec, smem_spec, vmem_spec],
        out_specs=(any_spec, any_spec),
        scratch_shapes=[
            pltpu.VMEM((MEMBERS, CHUNK, 128), BF16),
            pltpu.VMEM((MEMBERS, CHUNK, 128), BF16),
            pltpu.VMEM((RAW, 128), BF16),
            pltpu.VMEM((RAW, 128), F32),
            pltpu.VMEM((CHUNK, 128), F32),
            pltpu.VMEM((2, CHANS, LONS), BF16),
            pltpu.VMEM((CHANS, TAPS), BF16),
            pltpu.VMEM((4, 3, PAD_VARS, LONS), BF16),
            pltpu.VMEM((2, CHANS, LONS), BF16),
            pltpu.VMEM((2, TAPS, 128), F32),
            pltpu.VMEM((TAPS, 128), F32),
            pltpu.VMEM((ROWS, 128), BF16),
            pltpu.VMEM((CHIPS, PIECE, 128), BF16),
            pltpu.VMEM((5, PIECE, 128), BF16),
            pltpu.VMEM((4, PIECE, 128), BF16),
            dma, dma, dma, dma, dma((2,)), dma((2,)), dma, dma,
            dma, dma, dma, dma, dma, dma, dma, dma, dma, dma,
            dma((3,)), dma,
        ],
        compiler_params=pltpu.CompilerParams(
            collective_id=0, has_side_effects=True, vmem_limit_bytes=32 * 1024 * 1024
        ),
        name="crps_backward",
    )(members, obs, feats, weight, lat_weight, var_weight, land)
    feature_grad = fg.transpose(1, 0, 2)[None, None]
    factor = 1.0 / math.sqrt(2 * MEMBERS * 32 * LONS)
    flat = gw.reshape(2, ROWS, 128)[:, :TAPS].reshape(2, 9, PAD_VARS, 128)[:, ::-1, :VARS]
    grad_weight = flat.transpose(1, 2, 0, 3).reshape(9, VARS, CHANS).astype(F32) * factor
    return (feature_grad, grad_weight)


def solution(mesh):
    return jax.shard_map(
        local,
        mesh=mesh,
        in_specs=(
            P("dp", "ens", None, "lat", None),
            P("dp", "ens", None, "lat", None),
            P("dp", None, "lat", None),
            P(),
            P("lat"),
            P(),
            P("lat", None),
        ),
        out_specs=(P("dp", "ens", None, "lat", None), P()),
        check_vma=False,
    )
```

```python
import math

import jax
import jax.numpy as jnp
from jax import lax
from jax.experimental import pallas as pl
from jax.experimental.pallas import tpu as pltpu
from jax.sharding import PartitionSpec as P

MESH = pl.DeviceIdType.MESH
BF16 = jnp.bfloat16
F32 = jnp.float32

MEMBERS = 16
BANDS = 16
VARS = 72
PAD_VARS = 80
LONS = 512
CHANS = 256
OWNERS = 12
CHUNK = 48
RAW = VARS * 8
TAP_ROWS = 9 * VARS
PIECES = 21
PIECE = 32
STEPS = sorted(
    ((dx, dy) for dx in range(4) for dy in range(4)),
    key=lambda s: -(min(s[0], 4 - s[0]) + min(s[1], 4 - s[1])),
)


def kernel(
    members_ref, obs_ref, feats_ref, weight_ref, lat_ref, var_ref, land_ref,
    fg_ref, gw_ref,
    mbuf, obuf, gbuf, gf, obs, lats, vars_, land, fraw, ff, fs, wraw, weight, stack, wg, wgin, pieces, rs, zb, total,
    exch_send, exch_recv, back_send, back_recv, feat_send, feat_recv, halo_send, halo_recv, core_send, core_recv,
    rs_send, rs_recv, zb_send, zb_recv, ag_send, ag_recv, fwd_send, fwd_recv, load_sem,
    dp_in, one_in, two_in, four_in,
):
    ens = lax.axis_index("ens")
    lat = lax.axis_index("lat")
    dp = lax.axis_index("dp")
    core = lax.rem(ens, 2)
    x = lax.rem(ens, 8) // 2
    ylo = ens // 8
    y = dp * 2 + ylo
    up = lax.rem(lat + 1, BANDS)
    down = lax.rem(lat + BANDS - 1, BANDS)
    parity = lax.rem(lat, 2)
    pair = lat + 1 - 2 * parity
    other_core = ens + 1 - 2 * core

    def band(step):
        return lax.rem(lat + step, BANDS)

    def tell(sem, device):
        pl.semaphore_signal(sem, inc=1, device_id=device, device_id_type=MESH)

    barrier = pltpu.get_barrier_semaphore()

    def greet(k, c):
        tell(barrier, (lax.rem(ens + k, MEMBERS), lat, dp))
        return c

    lax.fori_loop(1, MEMBERS, greet, 0)
    tell(barrier, (ens, up, dp))
    tell(barrier, (ens, down, dp))
    tell(barrier, (ens, lat, 1 - dp))

    def chunk_of(e):
        pos = lax.rem(e, 4)
        first = jnp.where(e < 8, 1, 3)
        owns = pos != first
        return owns, (e // 4) * 3 + pos - jnp.where(pos > first, 1, 0)

    owned, mine = chunk_of(ens)
    mine = jnp.where(owned, mine, 0)

    loads = [
        pltpu.make_async_copy(src, dst, load_sem.at[i])
        for i, (src, dst) in enumerate((
            (feats_ref, fraw),
            (obs_ref.at[pl.ds(mine * CHUNK, CHUNK)], obs),
            (weight_ref, wraw),
            (land_ref, land),
            (lat_ref, lats),
            (var_ref, vars_),
        ))
    ]
    for load in loads:
        load.start()

    pl.semaphore_wait(barrier, 15 + 3)

    for dx, dy in STEPS:
        if dy > 1:
            continue
        for dc in range(2):
            if dx == dy == dc == 0:
                continue
            to = lax.rem(ylo + dy, 2) * 8 + lax.rem(x + dx, 4) * 2 + lax.rem(core + dc, 2)
            owns, chunk = chunk_of(to)

            @pl.when(owns)
            def _(to=to, chunk=chunk):
                pltpu.make_async_remote_copy(
                    src_ref=members_ref.at[pl.ds(chunk * CHUNK, CHUNK)], dst_ref=mbuf.at[ens],
                    send_sem=exch_send, recv_sem=exch_recv,
                    device_id=(to, lat, dp), device_id_type=MESH,
                ).start()

    @pl.when(owned)
    def _():
        pltpu.make_async_copy(members_ref.at[pl.ds(mine * CHUNK, CHUNK)], mbuf.at[ens], exch_recv).start()

    tell(dp_in, (ens, lat, 1 - dp))

    loads[0].wait()
    ff[...] = fraw[...].astype(F32)
    rows_out = []
    for r in range(2):
        for l in range(4):
            fs[r + 1, :, l * 128:(l + 1) * 128] = ff[pl.ds(2 * l + r, CHANS, stride=8), :].astype(BF16)
        rows_out.append(pltpu.make_async_remote_copy(
            src_ref=fs.at[r + 1], dst_ref=fs.at[3 - 3 * r],
            send_sem=feat_send.at[r], recv_sem=feat_recv.at[r],
            device_id=(ens, down if r == 0 else up, dp), device_id_type=MESH,
        ))
        rows_out[r].start()
    for load in loads[1:]:
        load.wait()

    @pl.when(owned)
    def _():
        pltpu.make_async_copy(mbuf, mbuf, exch_recv).wait()

        one = jnp.ones((16, 128), F32)
        zero = jnp.zeros((16, 128), F32)
        row = lax.broadcasted_iota(jnp.int32, (8, 128), 0)
        lat_rows = jnp.where(lax.rem(row, 2) == 0, lats[0], lats[1])
        land_rows = 1.0 + land[...].astype(F32)

        def tile(u, c):
            rows = pl.ds(pl.multiple_of(u * 16, 16), 16)
            vals = [mbuf[m, rows, :].astype(F32) for m in range(MEMBERS)]
            sums = [None] * MEMBERS
            for i in range(MEMBERS):
                for j in range(i + 1, MEMBERS):
                    s = jnp.where(vals[i] > vals[j], one, jnp.where(vals[i] < vals[j], -one, zero))
                    sums[i] = s if sums[i] is None else sums[i] + s
                    sums[j] = -s if sums[j] is None else sums[j] - s
            seen = obs[rows, :]
            v0 = mine * 6 + u * 2
            cell = jnp.concatenate(
                [(lat_rows * vars_[v0]) * land_rows, (lat_rows * vars_[v0 + 1]) * land_rows], axis=0
            )
            for m in range(MEMBERS):
                s = jnp.where(vals[m] > seen, one, jnp.where(vals[m] < seen, -one, zero))
                obuf[m, rows, :] = (cell * (s - sums[m] / (MEMBERS - 1))).astype(BF16)
            return c

        lax.fori_loop(0, CHUNK // 16, tile, 0)

        for dx, dy in STEPS:
            if dy > 1:
                continue
            for dc in range(2):
                if dx == dy == dc == 0:
                    continue
                to = lax.rem(ylo + dy, 2) * 8 + lax.rem(x + dx, 4) * 2 + lax.rem(core + dc, 2)
                pltpu.make_async_remote_copy(
                    src_ref=obuf.at[to], dst_ref=gbuf.at[pl.ds(mine * CHUNK, CHUNK)],
                    send_sem=back_send, recv_sem=back_recv,
                    device_id=(to, lat, dp), device_id_type=MESH,
                ).start()
        pltpu.make_async_copy(obuf.at[ens], gbuf.at[pl.ds(mine * CHUNK, CHUNK)], back_recv).start()

    pl.semaphore_wait(dp_in, 1)
    tell(one_in, (ens, up, dp))
    tell(one_in, (ens, down, dp))

    for t in range(9):
        taps = jnp.concatenate(
            [wraw[8 - t].astype(F32), jnp.zeros((PAD_VARS - VARS, CHANS), F32)], axis=0
        )
        weight[t * PAD_VARS:(t + 1) * PAD_VARS, :] = taps.astype(BF16)

    pltpu.make_async_copy(gbuf, gbuf, back_recv).wait()

    col = lax.broadcasted_iota(jnp.int32, (PAD_VARS, LONS), 1)

    def shifts(slot, v):
        stack[slot, 0] = jnp.where(col == 0, 0.0, pltpu.roll(v, 1, 1)).astype(BF16)
        stack[slot, 2] = jnp.where(col == LONS - 1, 0.0, pltpu.roll(v, LONS - 1, 1)).astype(BF16)

    gf[...] = gbuf[...].astype(F32)
    halo = []
    for r in range(2):
        v = jnp.concatenate([gf[pl.ds(2 * l + r, VARS, stride=8), :] for l in range(4)], axis=1)
        v = jnp.concatenate([v, jnp.zeros((PAD_VARS - VARS, LONS), F32)], axis=0)
        stack[r + 1, 1] = v.astype(BF16)
        halo.append(pltpu.make_async_remote_copy(
            src_ref=stack.at[r + 1, 1], dst_ref=stack.at[3 - 3 * r, 1],
            send_sem=halo_send.at[r], recv_sem=halo_recv.at[r],
            device_id=(ens, down if r == 0 else up, dp), device_id_type=MESH,
        ))
        halo[r].start()
        shifts(r + 1, v)
    pl.semaphore_wait(one_in, 2)
    tell(two_in, (ens, band(2), dp))
    tell(two_in, (ens, band(BANDS - 2), dp))

    def half(out, h, a):
        acc = None
        for r in range(2):
            part = lax.dot_general(
                stack[r + 1].reshape(3 * PAD_VARS, LONS),
                fs[r + 1 + a, pl.ds(pl.multiple_of(h * 128, 128), 128), :],
                (((1,), (1,)), ((), ())), preferred_element_type=F32,
            )
            acc = part if acc is None else acc + part
        for b in range(3):
            wg[out, a + 1, (2 - b) * VARS:(3 - b) * VARS, :] = acc[b * PAD_VARS:b * PAD_VARS + VARS, :]

    to_core = []
    for a in (0, -1, 1):
        if a:
            rows_out[(1 + a) // 2 ^ 1].wait_recv()

            @pl.when(lat == (0 if a < 0 else BANDS - 1))
            def _(a=a):
                fs[0 if a < 0 else 3] = jnp.zeros((CHANS, LONS), BF16)

        half(0, 1 - core, a)
        copy = pltpu.make_async_remote_copy(
            src_ref=wg.at[0, a + 1], dst_ref=wgin.at[a + 1], send_sem=core_send.at[a + 1], recv_sem=core_recv.at[a + 1],
            device_id=(other_core, lat, dp), device_id_type=MESH,
        )
        copy.start()
        to_core.append(copy)
    for a in (0, -1, 1):
        half(1, core, a)
    pl.semaphore_wait(two_in, 2)
    tell(four_in, (ens, band(4), dp))
    tell(four_in, (ens, band(BANDS - 4), dp))
    for copy in to_core:
        copy.wait_recv()
    mine_sum = (wg[1] + wgin[...]).reshape(TAP_ROWS, 128)
    fill = jnp.zeros((PIECES * PIECE - TAP_ROWS, 128), F32)
    pieces[...] = jnp.concatenate([mine_sum, fill], axis=0).astype(BF16)

    def piece_of(chip, par):
        first = lax.rem(lax.rem(chip, 4) + chip // 4, 2) == par
        second = jnp.logical_and(lax.rem(chip, 3) == 0, chip < 15)
        return jnp.logical_or(first, second), jnp.where(first, chip, 16 + chip // 3)

    spots = []
    for dz in (1, 0):
        for dx, dy in STEPS:
            if dx == dy == dz == 0:
                continue
            qx = lax.rem(x + dx, 4)
            qy = lax.rem(y + dy, 4)
            par = parity if dz == 0 else 1 - parity
            device = (lax.rem(qy, 2) * 8 + qx * 2 + core, lat if dz == 0 else pair, qy // 2)
            spots.append((qy * 4 + qx, par, device))
    place = (y * 4 + x) * 2 + parity
    sums, piece = piece_of(y * 4 + x, parity)
    piece = jnp.where(sums, piece, 0)
    for chip, par, device in spots:
        theirs, q = piece_of(chip, par)

        @pl.when(theirs)
        def _(q=q, device=device):
            pltpu.make_async_remote_copy(
                src_ref=pieces.at[pl.ds(q * PIECE, PIECE)], dst_ref=rs.at[place],
                send_sem=rs_send, recv_sem=rs_recv, device_id=device, device_id_type=MESH,
            ).start()

    @pl.when(sums)
    def _():
        pltpu.make_async_copy(pieces.at[pl.ds(piece * PIECE, PIECE)], rs.at[place], rs_recv).start()

    for r in range(2):
        halo[r].wait_recv()
    for slot, edge in ((3, BANDS - 1), (0, 0)):
        v = jnp.where(lat == edge, 0.0, stack[slot, 1].astype(F32))
        stack[slot, 1] = v.astype(BF16)
        shifts(slot, v)
    for r in range(2):
        grad = lax.dot_general(
            weight[...], stack[pl.ds(r, 3)].reshape(9 * PAD_VARS, LONS),
            (((0,), (0,)), ((), ())), preferred_element_type=F32,
        )
        for l in range(4):
            ff[pl.ds(2 * l + r, CHANS, stride=8), :] = grad[:, l * 128:(l + 1) * 128]
    fraw[...] = ff[...].astype(BF16)
    store = pltpu.make_async_copy(fraw, fg_ref, load_sem.at[0])
    store.start()

    pl.semaphore_wait(four_in, 2)

    @pl.when(sums)
    def _():
        pltpu.make_async_copy(rs, rs, rs_recv).wait()
        acc = rs[0].astype(F32)
        for q in range(1, 32):
            acc = acc + rs[q].astype(F32)
        zb[lat // 2] = acc.astype(BF16)
        for k in (8, 6, 10, 4, 12, 2, 14):
            pltpu.make_async_remote_copy(
                src_ref=zb.at[lat // 2], dst_ref=zb.at[lat // 2], send_sem=zb_send, recv_sem=zb_recv,
                device_id=(ens, band(k), dp), device_id_type=MESH,
            ).start()
        pltpu.make_async_copy(zb.at[pl.ds(0, 7)], zb.at[pl.ds(0, 7)], zb_recv).wait()
        acc = zb[0].astype(F32)
        for q in range(1, 8):
            acc = acc + zb[q].astype(F32)
        total[...] = acc.astype(BF16)
        for _, _, device in spots:
            pltpu.make_async_remote_copy(
                src_ref=total, dst_ref=gw_ref.at[core, piece],
                send_sem=ag_send, recv_sem=ag_recv, device_id=device, device_id_type=MESH,
            ).start()
        pltpu.make_async_copy(total, gw_ref.at[core, piece], ag_recv).start()

    pltpu.make_async_copy(gw_ref.at[core], gw_ref.at[core], ag_recv).wait()
    forward = pltpu.make_async_remote_copy(
        src_ref=gw_ref.at[core], dst_ref=gw_ref.at[core], send_sem=fwd_send, recv_sem=fwd_recv,
        device_id=(other_core, lat, dp), device_id_type=MESH,
    )
    forward.start()

    @pl.when(owned)
    def _():
        pltpu.make_async_copy(mbuf.at[pl.ds(0, OWNERS - 1)], mbuf.at[pl.ds(0, OWNERS - 1)], exch_send).wait()
        pltpu.make_async_copy(obuf.at[pl.ds(0, MEMBERS - 1)], obuf.at[pl.ds(0, MEMBERS - 1)], back_send).wait()

    @pl.when(jnp.logical_not(owned))
    def _():
        pltpu.make_async_copy(mbuf.at[pl.ds(0, OWNERS)], mbuf.at[pl.ds(0, OWNERS)], exch_send).wait()

    for r in range(2):
        rows_out[r].wait_send()
        halo[r].wait_send()
    for copy in to_core:
        copy.wait_send()

    @pl.when(sums)
    def _():
        pltpu.make_async_copy(rs.at[pl.ds(0, PIECES - 1)], rs.at[pl.ds(0, PIECES - 1)], rs_send).wait()
        pltpu.make_async_copy(zb.at[pl.ds(0, 7)], zb.at[pl.ds(0, 7)], zb_send).wait()
        pltpu.make_async_copy(rs.at[pl.ds(0, 31)], rs.at[pl.ds(0, 31)], ag_send).wait()

    @pl.when(jnp.logical_not(sums))
    def _():
        pltpu.make_async_copy(rs.at[pl.ds(0, PIECES)], rs.at[pl.ds(0, PIECES)], rs_send).wait()

    store.wait()
    forward.wait()


def write_results(factor, fg_ref, gw_ref, fg_out, gw_out, fgbuf, gwbuf, outbuf, sems, load_sem, fg_sems):
    load = pltpu.make_async_copy(gw_ref, gwbuf, load_sem)
    load.start()
    quarter = CHANS * 2
    parts = [pl.ds(i * quarter, quarter) for i in range(4)]
    loads = [pltpu.make_async_copy(fg_ref.at[p], fgbuf.at[p], fg_sems.at[i]) for i, p in enumerate(parts)]
    for copy in loads:
        copy.start()
    load.wait()
    copies = []
    for i in range(3):
        rows = pl.ds(i * 3 * VARS, 3 * VARS)
        for c in range(2):
            wide = gwbuf[c].reshape(PIECES * PIECE, 128).astype(F32)
            outbuf[rows, c * 128:(c + 1) * 128] = wide[i * 3 * VARS:(i + 1) * 3 * VARS] * factor
        copies.append(pltpu.make_async_copy(outbuf.at[rows], gw_out.at[rows], sems.at[i]))
        copies[i].start()
    for i, p in enumerate(parts):
        loads[i].wait()
        copies.append(pltpu.make_async_copy(fgbuf.at[p], fg_out.at[p], sems.at[3 + i]))
        copies[-1].start()
    for copy in copies:
        copy.wait()


def raw_rows(v):
    lead = v.shape[0]
    return v.reshape(lead, 2, 4, 128).transpose(0, 2, 1, 3).reshape(lead * 8, 128)


def local(features, members_out, observed, conv_weight, lat_weight, var_weight, land_mask):
    hbm = pl.BlockSpec(memory_space=pltpu.HBM)
    anywhere = pl.BlockSpec(memory_space=pl.ANY)
    dma = pltpu.SemaphoreType.DMA
    regular = pltpu.SemaphoreType.REGULAR
    fg, gw = pl.pallas_call(
        kernel,
        out_shape=(
            jax.ShapeDtypeStruct((CHANS * 8, 128), BF16),
            jax.ShapeDtypeStruct((2, PIECES, PIECE, 128), BF16),
        ),
        in_specs=[hbm] * 7,
        out_specs=(anywhere, anywhere),
        scratch_shapes=[
            pltpu.VMEM((MEMBERS, CHUNK, 128), BF16),
            pltpu.VMEM((MEMBERS, CHUNK, 128), BF16),
            pltpu.VMEM((RAW, 128), BF16),
            pltpu.VMEM((RAW, 128), F32),
            pltpu.VMEM((CHUNK, 128), F32),
            pltpu.SMEM((2,), F32),
            pltpu.SMEM((VARS,), F32),
            pltpu.VMEM((8, 128), jnp.int32),
            pltpu.VMEM((CHANS * 8, 128), BF16),
            pltpu.VMEM((CHANS * 8, 128), F32),
            pltpu.VMEM((4, CHANS, LONS), BF16),
            pltpu.VMEM((9, VARS, CHANS), BF16),
            pltpu.VMEM((9 * PAD_VARS, CHANS), BF16),
            pltpu.VMEM((4, 3, PAD_VARS, LONS), BF16),
            pltpu.VMEM((2, 3, 3 * VARS, 128), F32),
            pltpu.VMEM((3, 3 * VARS, 128), F32),
            pltpu.VMEM((PIECES * PIECE, 128), BF16),
            pltpu.VMEM((32, PIECE, 128), BF16),
            pltpu.VMEM((8, PIECE, 128), BF16),
            pltpu.VMEM((PIECE, 128), BF16),
            dma, dma, dma, dma, dma((2,)), dma((2,)), dma((2,)), dma((2,)), dma((3,)), dma((3,)),
            dma, dma, dma, dma, dma, dma, dma, dma, dma((6,)),
            regular, regular, regular, regular,
        ],
        compiler_params=pltpu.CompilerParams(
            collective_id=0, has_side_effects=True, vmem_limit_bytes=60 * 1024 * 1024
        ),
        name="crps_backward",
    )(
        raw_rows(members_out[0, 0]), raw_rows(observed[0]), raw_rows(features[0, 0]), conv_weight,
        lat_weight, var_weight, raw_rows(land_mask[None]),
    )
    factor = 1.0 / math.sqrt(2 * MEMBERS * 32 * LONS)

    def body(*refs):
        write_results(factor, *refs)

    feature_grad, grad_weight = pl.pallas_call(
        body,
        out_shape=(
            jax.ShapeDtypeStruct((CHANS * 8, 128), BF16),
            jax.ShapeDtypeStruct((TAP_ROWS, CHANS), F32),
        ),
        in_specs=[anywhere, anywhere],
        out_specs=(hbm, hbm),
        scratch_shapes=[
            pltpu.VMEM((CHANS * 8, 128), BF16),
            pltpu.VMEM((2, PIECES, PIECE, 128), BF16),
            pltpu.VMEM((TAP_ROWS, CHANS), F32),
            dma((7,)), dma, dma((4,)),
        ],
        compiler_params=pltpu.CompilerParams(vmem_limit_bytes=60 * 1024 * 1024),
        name="write_results",
    )(fg, gw)
    feature_grad = feature_grad.reshape(CHANS, 4, 2, 128).transpose(0, 2, 1, 3).reshape(1, 1, CHANS, 2, LONS)
    return (feature_grad, grad_weight.reshape(9, VARS, CHANS))


def solution(mesh):
    return jax.shard_map(
        local,
        mesh=mesh,
        in_specs=(
            P("dp", "ens", None, "lat", None),
            P("dp", "ens", None, "lat", None),
            P("dp", None, "lat", None),
            P(),
            P("lat"),
            P(),
            P("lat", None),
        ),
        out_specs=(P("dp", "ens", None, "lat", None), P()),
        check_vma=False,
    )
```

```python
import math

import jax
import jax.numpy as jnp
from jax import lax
from jax.experimental import pallas as pl
from jax.experimental.pallas import tpu as pltpu
from jax.sharding import PartitionSpec as P

MESH = pl.DeviceIdType.MESH
BF16 = jnp.bfloat16
F32 = jnp.float32

MEMBERS = 16
BANDS = 16
VARS = 72
PAD_VARS = 80
LONS = 512
CHANS = 256
OWNERS = 12
CHUNK = 48
RAW = VARS * 8
TAP_ROWS = 9 * VARS
PIECES = 21
PIECE = 32
STEPS = sorted(
    ((dx, dy) for dx in range(4) for dy in range(4)),
    key=lambda s: -(min(s[0], 4 - s[0]) + min(s[1], 4 - s[1])),
)


def kernel(
    members_ref, obs_ref, feats_ref, weight_ref, lat_ref, var_ref, land_ref,
    fg_ref, gw_ref,
    members, mbuf, obuf, gbuf, gf, obs, lats, vars_, land, fraw, ff, fs, wraw, weight, stack, wg, wgin, pieces, rs, zb, total,
    exch_send, exch_recv, back_send, back_recv, feat_send, feat_recv, halo_send, halo_recv, core_send, core_recv,
    rs_send, rs_recv, zb_send, zb_recv, ag_send, ag_recv, fwd_send, fwd_recv, load_sem,
    dp_in, pair_in, one_in, two_in, four_in,
):
    ens = lax.axis_index("ens")
    lat = lax.axis_index("lat")
    dp = lax.axis_index("dp")
    core = lax.rem(ens, 2)
    x = lax.rem(ens, 8) // 2
    ylo = ens // 8
    y = dp * 2 + ylo
    up = lax.rem(lat + 1, BANDS)
    down = lax.rem(lat + BANDS - 1, BANDS)
    parity = lax.rem(lat, 2)
    pair = lat + 1 - 2 * parity
    other_core = ens + 1 - 2 * core

    def band(step):
        return lax.rem(lat + step, BANDS)

    def tell(sem, device):
        pl.semaphore_signal(sem, inc=1, device_id=device, device_id_type=MESH)

    barrier = pltpu.get_barrier_semaphore()

    def greet(k, c):
        tell(barrier, (lax.rem(ens + k, MEMBERS), lat, dp))
        return c

    lax.fori_loop(1, MEMBERS, greet, 0)
    tell(barrier, (ens, up, dp))
    tell(barrier, (ens, down, dp))
    tell(barrier, (ens, lat, 1 - dp))

    def chunk_of(e):
        pos = lax.rem(e, 4)
        first = jnp.where(e < 8, 1, 3)
        owns = pos != first
        return owns, (e // 4) * 3 + pos - jnp.where(pos > first, 1, 0)

    owned, mine = chunk_of(ens)
    mine = jnp.where(owned, mine, 0)

    loads = [
        pltpu.make_async_copy(src, dst, load_sem.at[i])
        for i, (src, dst) in enumerate((
            (members_ref, members),
            (feats_ref, fraw),
            (obs_ref.at[pl.ds(mine * CHUNK, CHUNK)], obs),
            (weight_ref, wraw),
            (land_ref, land),
            (lat_ref, lats),
            (var_ref, vars_),
        ))
    ]
    for load in loads:
        load.start()
    loads[0].wait()

    pl.semaphore_wait(barrier, 15 + 3)

    for dx, dy in STEPS:
        if dy > 1:
            continue
        for dc in range(2):
            if dx == dy == dc == 0:
                continue
            to = lax.rem(ylo + dy, 2) * 8 + lax.rem(x + dx, 4) * 2 + lax.rem(core + dc, 2)
            owns, chunk = chunk_of(to)

            @pl.when(owns)
            def _(to=to, chunk=chunk):
                pltpu.make_async_remote_copy(
                    src_ref=members.at[pl.ds(chunk * CHUNK, CHUNK)], dst_ref=mbuf.at[ens],
                    send_sem=exch_send, recv_sem=exch_recv,
                    device_id=(to, lat, dp), device_id_type=MESH,
                ).start()

    @pl.when(owned)
    def _():
        pltpu.make_async_copy(members.at[pl.ds(mine * CHUNK, CHUNK)], mbuf.at[ens], exch_recv).start()

    tell(dp_in, (ens, lat, 1 - dp))
    tell(one_in, (ens, up, dp))
    tell(one_in, (ens, down, dp))

    loads[1].wait()
    ff[...] = fraw[...].astype(F32)
    rows_out = []
    for r in range(2):
        for l in range(4):
            fs[r + 1, :, l * 128:(l + 1) * 128] = ff[pl.ds(2 * l + r, CHANS, stride=8), :].astype(BF16)
        rows_out.append(pltpu.make_async_remote_copy(
            src_ref=fs.at[r + 1], dst_ref=fs.at[3 - 3 * r],
            send_sem=feat_send.at[r], recv_sem=feat_recv.at[r],
            device_id=(ens, down if r == 0 else up, dp), device_id_type=MESH,
        ))
        rows_out[r].start()
    for load in loads[2:]:
        load.wait()
    pl.semaphore_wait(one_in, 2)
    tell(two_in, (ens, band(2), dp))
    tell(two_in, (ens, band(BANDS - 2), dp))

    @pl.when(owned)
    def _():
        pltpu.make_async_copy(mbuf, mbuf, exch_recv).wait()

        one = jnp.ones((16, 128), F32)
        zero = jnp.zeros((16, 128), F32)
        row = lax.broadcasted_iota(jnp.int32, (8, 128), 0)
        lat_rows = jnp.where(lax.rem(row, 2) == 0, lats[0], lats[1])
        land_rows = 1.0 + land[...].astype(F32)

        def tile(u, c):
            rows = pl.ds(pl.multiple_of(u * 16, 16), 16)
            vals = [mbuf[m, rows, :].astype(F32) for m in range(MEMBERS)]
            sums = [None] * MEMBERS
            for i in range(MEMBERS):
                for j in range(i + 1, MEMBERS):
                    s = jnp.where(vals[i] > vals[j], one, jnp.where(vals[i] < vals[j], -one, zero))
                    sums[i] = s if sums[i] is None else sums[i] + s
                    sums[j] = -s if sums[j] is None else sums[j] - s
            seen = obs[rows, :]
            v0 = mine * 6 + u * 2
            cell = jnp.concatenate(
                [(lat_rows * vars_[v0]) * land_rows, (lat_rows * vars_[v0 + 1]) * land_rows], axis=0
            )
            for m in range(MEMBERS):
                s = jnp.where(vals[m] > seen, one, jnp.where(vals[m] < seen, -one, zero))
                obuf[m, rows, :] = (cell * (s - sums[m] / (MEMBERS - 1))).astype(BF16)
            return c

        lax.fori_loop(0, CHUNK // 16, tile, 0)

        for dx, dy in STEPS:
            if dy > 1:
                continue
            for dc in range(2):
                if dx == dy == dc == 0:
                    continue
                to = lax.rem(ylo + dy, 2) * 8 + lax.rem(x + dx, 4) * 2 + lax.rem(core + dc, 2)
                pltpu.make_async_remote_copy(
                    src_ref=obuf.at[to], dst_ref=gbuf.at[pl.ds(mine * CHUNK, CHUNK)],
                    send_sem=back_send, recv_sem=back_recv,
                    device_id=(to, lat, dp), device_id_type=MESH,
                ).start()
        pltpu.make_async_copy(obuf.at[ens], gbuf.at[pl.ds(mine * CHUNK, CHUNK)], back_recv).start()

    pl.semaphore_wait(dp_in, 1)
    tell(pair_in, (ens, pair, dp))
    pl.semaphore_wait(two_in, 2)
    tell(four_in, (ens, band(4), dp))
    tell(four_in, (ens, band(BANDS - 4), dp))

    for t in range(9):
        taps = jnp.concatenate(
            [wraw[8 - t].astype(F32), jnp.zeros((PAD_VARS - VARS, CHANS), F32)], axis=0
        )
        weight[t * PAD_VARS:(t + 1) * PAD_VARS, :] = taps.astype(BF16)

    pltpu.make_async_copy(gbuf, gbuf, back_recv).wait()

    col = lax.broadcasted_iota(jnp.int32, (PAD_VARS, LONS), 1)

    def shifts(slot, v):
        stack[slot, 0] = jnp.where(col == 0, 0.0, pltpu.roll(v, 1, 1)).astype(BF16)
        stack[slot, 2] = jnp.where(col == LONS - 1, 0.0, pltpu.roll(v, LONS - 1, 1)).astype(BF16)

    gf[...] = gbuf[...].astype(F32)
    halo = []
    for r in range(2):
        v = jnp.concatenate([gf[pl.ds(2 * l + r, VARS, stride=8), :] for l in range(4)], axis=1)
        v = jnp.concatenate([v, jnp.zeros((PAD_VARS - VARS, LONS), F32)], axis=0)
        stack[r + 1, 1] = v.astype(BF16)
        halo.append(pltpu.make_async_remote_copy(
            src_ref=stack.at[r + 1, 1], dst_ref=stack.at[3 - 3 * r, 1],
            send_sem=halo_send.at[r], recv_sem=halo_recv.at[r],
            device_id=(ens, down if r == 0 else up, dp), device_id_type=MESH,
        ))
        halo[r].start()
        shifts(r + 1, v)

    def half(out, h, a):
        acc = None
        for r in range(2):
            part = lax.dot_general(
                stack[r + 1].reshape(3 * PAD_VARS, LONS),
                fs[r + 1 + a, pl.ds(pl.multiple_of(h * 128, 128), 128), :],
                (((1,), (1,)), ((), ())), preferred_element_type=F32,
            )
            acc = part if acc is None else acc + part
        for b in range(3):
            wg[out, a + 1, (2 - b) * VARS:(3 - b) * VARS, :] = acc[b * PAD_VARS:b * PAD_VARS + VARS, :]

    to_core = []
    for a in (0, -1, 1):
        if a:
            rows_out[(1 + a) // 2 ^ 1].wait_recv()

            @pl.when(lat == (0 if a < 0 else BANDS - 1))
            def _(a=a):
                fs[0 if a < 0 else 3] = jnp.zeros((CHANS, LONS), BF16)

        half(0, 1 - core, a)
        copy = pltpu.make_async_remote_copy(
            src_ref=wg.at[0, a + 1], dst_ref=wgin.at[a + 1], send_sem=core_send.at[a + 1], recv_sem=core_recv.at[a + 1],
            device_id=(other_core, lat, dp), device_id_type=MESH,
        )
        copy.start()
        to_core.append(copy)
    for a in (0, -1, 1):
        half(1, core, a)
    pl.semaphore_wait(pair_in, 1)
    for copy in to_core:
        copy.wait_recv()
    mine_sum = (wg[1] + wgin[...]).reshape(TAP_ROWS, 128)
    fill = jnp.zeros((PIECES * PIECE - TAP_ROWS, 128), F32)
    pieces[...] = jnp.concatenate([mine_sum, fill], axis=0).astype(BF16)

    def piece_of(chip, par):
        first = lax.rem(lax.rem(chip, 4) + chip // 4, 2) == par
        second = jnp.logical_and(lax.rem(chip, 3) == 0, chip < 15)
        return jnp.logical_or(first, second), jnp.where(first, chip, 16 + chip // 3)

    spots = []
    for dz in (1, 0):
        for dx, dy in STEPS:
            if dx == dy == dz == 0:
                continue
            qx = lax.rem(x + dx, 4)
            qy = lax.rem(y + dy, 4)
            par = parity if dz == 0 else 1 - parity
            device = (lax.rem(qy, 2) * 8 + qx * 2 + core, lat if dz == 0 else pair, qy // 2)
            spots.append((qy * 4 + qx, par, device))
    place = (y * 4 + x) * 2 + parity
    sums, piece = piece_of(y * 4 + x, parity)
    piece = jnp.where(sums, piece, 0)
    for chip, par, device in spots:
        theirs, q = piece_of(chip, par)

        @pl.when(theirs)
        def _(q=q, device=device):
            pltpu.make_async_remote_copy(
                src_ref=pieces.at[pl.ds(q * PIECE, PIECE)], dst_ref=rs.at[place],
                send_sem=rs_send, recv_sem=rs_recv, device_id=device, device_id_type=MESH,
            ).start()

    @pl.when(sums)
    def _():
        pltpu.make_async_copy(pieces.at[pl.ds(piece * PIECE, PIECE)], rs.at[place], rs_recv).start()

    for r in range(2):
        halo[r].wait_recv()
    for slot, edge in ((3, BANDS - 1), (0, 0)):
        v = jnp.where(lat == edge, 0.0, stack[slot, 1].astype(F32))
        stack[slot, 1] = v.astype(BF16)
        shifts(slot, v)
    for r in range(2):
        grad = lax.dot_general(
            weight[...], stack[pl.ds(r, 3)].reshape(9 * PAD_VARS, LONS),
            (((0,), (0,)), ((), ())), preferred_element_type=F32,
        )
        for l in range(4):
            ff[pl.ds(2 * l + r, CHANS, stride=8), :] = grad[:, l * 128:(l + 1) * 128]
    fg_ref[...] = ff[...].astype(BF16)

    pl.semaphore_wait(four_in, 2)

    @pl.when(sums)
    def _():
        pltpu.make_async_copy(rs, rs, rs_recv).wait()
        acc = rs[0].astype(F32)
        for q in range(1, 32):
            acc = acc + rs[q].astype(F32)
        zb[lat // 2] = acc.astype(BF16)
        for k in (8, 6, 10, 4, 12, 2, 14):
            pltpu.make_async_remote_copy(
                src_ref=zb.at[lat // 2], dst_ref=zb.at[lat // 2], send_sem=zb_send, recv_sem=zb_recv,
                device_id=(ens, band(k), dp), device_id_type=MESH,
            ).start()
        pltpu.make_async_copy(zb.at[pl.ds(0, 7)], zb.at[pl.ds(0, 7)], zb_recv).wait()
        acc = zb[0].astype(F32)
        for q in range(1, 8):
            acc = acc + zb[q].astype(F32)
        total[...] = acc.astype(BF16)
        for _, _, device in spots:
            pltpu.make_async_remote_copy(
                src_ref=total, dst_ref=gw_ref.at[core, piece],
                send_sem=ag_send, recv_sem=ag_recv, device_id=device, device_id_type=MESH,
            ).start()
        pltpu.make_async_copy(total, gw_ref.at[core, piece], ag_recv).start()

    pltpu.make_async_copy(gw_ref.at[core], gw_ref.at[core], ag_recv).wait()
    forward = pltpu.make_async_remote_copy(
        src_ref=gw_ref.at[core], dst_ref=gw_ref.at[core], send_sem=fwd_send, recv_sem=fwd_recv,
        device_id=(other_core, lat, dp), device_id_type=MESH,
    )
    forward.start()

    @pl.when(owned)
    def _():
        pltpu.make_async_copy(mbuf.at[pl.ds(0, OWNERS - 1)], mbuf.at[pl.ds(0, OWNERS - 1)], exch_send).wait()
        pltpu.make_async_copy(obuf.at[pl.ds(0, MEMBERS - 1)], obuf.at[pl.ds(0, MEMBERS - 1)], back_send).wait()

    @pl.when(jnp.logical_not(owned))
    def _():
        pltpu.make_async_copy(mbuf.at[pl.ds(0, OWNERS)], mbuf.at[pl.ds(0, OWNERS)], exch_send).wait()

    for r in range(2):
        rows_out[r].wait_send()
        halo[r].wait_send()
    for copy in to_core:
        copy.wait_send()

    @pl.when(sums)
    def _():
        pltpu.make_async_copy(rs.at[pl.ds(0, PIECES - 1)], rs.at[pl.ds(0, PIECES - 1)], rs_send).wait()
        pltpu.make_async_copy(zb.at[pl.ds(0, 7)], zb.at[pl.ds(0, 7)], zb_send).wait()
        pltpu.make_async_copy(rs.at[pl.ds(0, 31)], rs.at[pl.ds(0, 31)], ag_send).wait()

    @pl.when(jnp.logical_not(sums))
    def _():
        pltpu.make_async_copy(rs.at[pl.ds(0, PIECES)], rs.at[pl.ds(0, PIECES)], rs_send).wait()

    forward.wait()


def write_results(factor, fg_ref, gw_ref, fg_out, gw_out, outbuf, sems):
    copies = [pltpu.make_async_copy(fg_ref, fg_out, sems.at[3])]
    copies[0].start()
    for i in range(3):
        rows = pl.ds(i * 3 * VARS, 3 * VARS)
        for c in range(2):
            wide = gw_ref[c].reshape(PIECES * PIECE, 128).astype(F32)
            outbuf[rows, c * 128:(c + 1) * 128] = wide[i * 3 * VARS:(i + 1) * 3 * VARS] * factor
        copies.append(pltpu.make_async_copy(outbuf.at[rows], gw_out.at[rows], sems.at[i]))
        copies[-1].start()
    for copy in copies:
        copy.wait()


def raw_rows(v):
    lead = v.shape[0]
    return v.reshape(lead, 2, 4, 128).transpose(0, 2, 1, 3).reshape(lead * 8, 128)


def local(features, members_out, observed, conv_weight, lat_weight, var_weight, land_mask):
    hbm = pl.BlockSpec(memory_space=pltpu.HBM)
    vmem = pl.BlockSpec(memory_space=pltpu.VMEM)
    dma = pltpu.SemaphoreType.DMA
    regular = pltpu.SemaphoreType.REGULAR
    fg, gw = pl.pallas_call(
        kernel,
        out_shape=(
            pltpu.VMEM((CHANS * 8, 128), BF16),
            pltpu.VMEM((2, PIECES, PIECE, 128), BF16),
        ),
        in_specs=[hbm] * 7,
        out_specs=(vmem, vmem),
        scratch_shapes=[
            pltpu.VMEM((RAW, 128), BF16),
            pltpu.VMEM((MEMBERS, CHUNK, 128), BF16),
            pltpu.VMEM((MEMBERS, CHUNK, 128), BF16),
            pltpu.VMEM((RAW, 128), BF16),
            pltpu.VMEM((RAW, 128), F32),
            pltpu.VMEM((CHUNK, 128), F32),
            pltpu.SMEM((2,), F32),
            pltpu.SMEM((VARS,), F32),
            pltpu.VMEM((8, 128), jnp.int32),
            pltpu.VMEM((CHANS * 8, 128), BF16),
            pltpu.VMEM((CHANS * 8, 128), F32),
            pltpu.VMEM((4, CHANS, LONS), BF16),
            pltpu.VMEM((9, VARS, CHANS), BF16),
            pltpu.VMEM((9 * PAD_VARS, CHANS), BF16),
            pltpu.VMEM((4, 3, PAD_VARS, LONS), BF16),
            pltpu.VMEM((2, 3, 3 * VARS, 128), F32),
            pltpu.VMEM((3, 3 * VARS, 128), F32),
            pltpu.VMEM((PIECES * PIECE, 128), BF16),
            pltpu.VMEM((32, PIECE, 128), BF16),
            pltpu.VMEM((8, PIECE, 128), BF16),
            pltpu.VMEM((PIECE, 128), BF16),
            dma, dma, dma, dma, dma((2,)), dma((2,)), dma((2,)), dma((2,)), dma((3,)), dma((3,)),
            dma, dma, dma, dma, dma, dma, dma, dma, dma((7,)),
            regular, regular, regular, regular, regular,
        ],
        compiler_params=pltpu.CompilerParams(
            collective_id=0, has_side_effects=True, vmem_limit_bytes=48 * 1024 * 1024
        ),
        name="crps_backward",
    )(*(
        pltpu.with_memory_space_constraint(v, pltpu.HBM)
        for v in (
            raw_rows(members_out[0, 0]), raw_rows(observed[0]), raw_rows(features[0, 0]), conv_weight,
            lat_weight, var_weight, raw_rows(land_mask[None]),
        )
    ))
    factor = 1.0 / math.sqrt(2 * MEMBERS * 32 * LONS)

    def body(*refs):
        write_results(factor, *refs)

    feature_grad, grad_weight = pl.pallas_call(
        body,
        out_shape=(
            jax.ShapeDtypeStruct((CHANS * 8, 128), BF16),
            jax.ShapeDtypeStruct((TAP_ROWS, CHANS), F32),
        ),
        in_specs=[vmem, vmem],
        out_specs=(hbm, hbm),
        scratch_shapes=[
            pltpu.VMEM((TAP_ROWS, CHANS), F32),
            dma((4,)),
        ],
        compiler_params=pltpu.CompilerParams(vmem_limit_bytes=48 * 1024 * 1024),
        name="write_results",
    )(*(pltpu.with_memory_space_constraint(v, pltpu.VMEM) for v in (fg, gw)))
    feature_grad = feature_grad.reshape(CHANS, 4, 2, 128).transpose(0, 2, 1, 3).reshape(1, 1, CHANS, 2, LONS)
    return (feature_grad, grad_weight.reshape(9, VARS, CHANS))


def solution(mesh):
    return jax.shard_map(
        local,
        mesh=mesh,
        in_specs=(
            P("dp", "ens", None, "lat", None),
            P("dp", "ens", None, "lat", None),
            P("dp", None, "lat", None),
            P(),
            P("lat"),
            P(),
            P("lat", None),
        ),
        out_specs=(P("dp", "ens", None, "lat", None), P()),
        check_vma=False,
    )
```

```python
import math

import jax
import jax.numpy as jnp
from jax import lax
from jax.experimental import pallas as pl
from jax.experimental.pallas import tpu as pltpu
from jax.sharding import PartitionSpec as P

MESH = pl.DeviceIdType.MESH
BF16 = jnp.bfloat16
F32 = jnp.float32

MEMBERS = 16
BANDS = 16
VARS = 72
PAD_VARS = 80
LONS = 512
CHANS = 256
OWNERS = 12
CHUNK = 48
RAW = VARS * 8
TAP_ROWS = 9 * VARS
PIECES = 21
PIECE = 32
STEPS = sorted(
    ((dx, dy) for dx in range(4) for dy in range(4)),
    key=lambda s: -(min(s[0], 4 - s[0]) + min(s[1], 4 - s[1])),
)


def div(v, n):
    return lax.shift_right_logical(v, n.bit_length() - 1)


def mod(v, n):
    return lax.bitwise_and(v, n - 1)


def third(v):
    return lax.shift_right_logical(v * 11, 5)


def kernel(
    members_ref, obs_ref, feats_ref, weight_ref, lat_ref, var_ref, land_ref,
    fg_ref, gw_ref,
    members, mbuf, obuf, gbuf, gf, obs, lats, vars_, land, fraw, ff, fs, wraw, weight, stack, wg, wgin, pieces, rs, zb, total,
    exch_send, exch_recv, back_send, back_recv, feat_send, feat_recv, halo_send, halo_recv, core_send, core_recv,
    rs_send, rs_recv, zb_send, zb_recv, ag_send, ag_recv, fwd_send, fwd_recv, load_sem,
    dp_in, pair_in, one_in, two_in, four_in,
):
    ens = lax.axis_index("ens")
    lat = lax.axis_index("lat")
    dp = lax.axis_index("dp")
    core = mod(ens, 2)
    x = div(mod(ens, 8), 2)
    ylo = div(ens, 8)
    y = dp * 2 + ylo
    up = mod(lat + 1, BANDS)
    down = mod(lat + BANDS - 1, BANDS)
    parity = mod(lat, 2)
    pair = lat + 1 - 2 * parity
    other_core = ens + 1 - 2 * core

    def band(step):
        return mod(lat + step, BANDS)

    def tell(sem, device):
        pl.semaphore_signal(sem, inc=1, device_id=device, device_id_type=MESH)

    barrier = pltpu.get_barrier_semaphore()

    for dx, dy in STEPS:
        for dc in range(2):
            if dy <= 1 and (dx or dy or dc):
                tell(barrier, (mod(ylo + dy, 2) * 8 + mod(x + dx, 4) * 2 + mod(core + dc, 2), lat, dp))
    tell(barrier, (ens, up, dp))
    tell(barrier, (ens, down, dp))
    tell(barrier, (ens, lat, 1 - dp))

    def chunk_of(e):
        pos = mod(e, 4)
        first = jnp.where(e < 8, 1, 3)
        owns = pos != first
        return owns, div(e, 4) * 3 + pos - jnp.where(pos > first, 1, 0)

    owned, mine = chunk_of(ens)
    mine = jnp.where(owned, mine, 0)

    loads = [
        pltpu.make_async_copy(src, dst, load_sem.at[i])
        for i, (src, dst) in enumerate((
            (members_ref, members),
            (feats_ref, fraw),
            (obs_ref.at[pl.ds(mine * CHUNK, CHUNK)], obs),
            (weight_ref, wraw),
            (land_ref, land),
            (lat_ref, lats),
            (var_ref, vars_),
        ))
    ]
    for load in loads:
        load.start()
    loads[0].wait()

    pl.semaphore_wait(barrier, 15 + 3)

    for dx, dy in STEPS:
        if dy > 1:
            continue
        for dc in range(2):
            if dx == dy == dc == 0:
                continue
            to = mod(ylo + dy, 2) * 8 + mod(x + dx, 4) * 2 + mod(core + dc, 2)
            owns, chunk = chunk_of(to)

            @pl.when(owns)
            def _(to=to, chunk=chunk):
                pltpu.make_async_remote_copy(
                    src_ref=members.at[pl.ds(chunk * CHUNK, CHUNK)], dst_ref=mbuf.at[ens],
                    send_sem=exch_send, recv_sem=exch_recv,
                    device_id=(to, lat, dp), device_id_type=MESH,
                ).start()

    @pl.when(owned)
    def _():
        pltpu.make_async_copy(members.at[pl.ds(mine * CHUNK, CHUNK)], mbuf.at[ens], exch_recv).start()

    tell(dp_in, (ens, lat, 1 - dp))
    tell(one_in, (ens, up, dp))
    tell(one_in, (ens, down, dp))

    loads[1].wait()
    ff[...] = fraw[...].astype(F32)
    rows_out = []
    for r in range(2):
        for l in range(4):
            fs[r + 1, :, l * 128:(l + 1) * 128] = ff[pl.ds(2 * l + r, CHANS, stride=8), :].astype(BF16)
        rows_out.append(pltpu.make_async_remote_copy(
            src_ref=fs.at[r + 1], dst_ref=fs.at[3 - 3 * r],
            send_sem=feat_send.at[r], recv_sem=feat_recv.at[r],
            device_id=(ens, down if r == 0 else up, dp), device_id_type=MESH,
        ))
        rows_out[r].start()
    for load in loads[2:]:
        load.wait()
    pl.semaphore_wait(one_in, 2)
    tell(two_in, (ens, band(2), dp))
    tell(two_in, (ens, band(BANDS - 2), dp))

    @pl.when(owned)
    def _():
        pltpu.make_async_copy(mbuf, mbuf, exch_recv).wait()

        one = jnp.ones((16, 128), F32)
        zero = jnp.zeros((16, 128), F32)
        row = lax.broadcasted_iota(jnp.int32, (8, 128), 0)
        lat_rows = jnp.where(lax.rem(row, 2) == 0, lats[0], lats[1])
        land_rows = 1.0 + land[...].astype(F32)

        def tile(u, c):
            rows = pl.ds(pl.multiple_of(u * 16, 16), 16)
            vals = [mbuf[m, rows, :].astype(F32) for m in range(MEMBERS)]
            sums = [None] * MEMBERS
            for i in range(MEMBERS):
                for j in range(i + 1, MEMBERS):
                    s = jnp.where(vals[i] > vals[j], one, jnp.where(vals[i] < vals[j], -one, zero))
                    sums[i] = s if sums[i] is None else sums[i] + s
                    sums[j] = -s if sums[j] is None else sums[j] - s
            seen = obs[rows, :]
            v0 = mine * 6 + u * 2
            cell = jnp.concatenate(
                [(lat_rows * vars_[v0]) * land_rows, (lat_rows * vars_[v0 + 1]) * land_rows], axis=0
            )
            for m in range(MEMBERS):
                s = jnp.where(vals[m] > seen, one, jnp.where(vals[m] < seen, -one, zero))
                obuf[m, rows, :] = (cell * (s - sums[m] / (MEMBERS - 1))).astype(BF16)
            return c

        lax.fori_loop(0, CHUNK // 16, tile, 0)

        for dx, dy in STEPS:
            if dy > 1:
                continue
            for dc in range(2):
                if dx == dy == dc == 0:
                    continue
                to = mod(ylo + dy, 2) * 8 + mod(x + dx, 4) * 2 + mod(core + dc, 2)
                pltpu.make_async_remote_copy(
                    src_ref=obuf.at[to], dst_ref=gbuf.at[pl.ds(mine * CHUNK, CHUNK)],
                    send_sem=back_send, recv_sem=back_recv,
                    device_id=(to, lat, dp), device_id_type=MESH,
                ).start()
        pltpu.make_async_copy(obuf.at[ens], gbuf.at[pl.ds(mine * CHUNK, CHUNK)], back_recv).start()

    pl.semaphore_wait(dp_in, 1)
    tell(pair_in, (ens, pair, dp))
    pl.semaphore_wait(two_in, 2)
    tell(four_in, (ens, band(4), dp))
    tell(four_in, (ens, band(BANDS - 4), dp))

    for t in range(9):
        taps = jnp.concatenate(
            [wraw[8 - t].astype(F32), jnp.zeros((PAD_VARS - VARS, CHANS), F32)], axis=0
        )
        weight[t * PAD_VARS:(t + 1) * PAD_VARS, :] = taps.astype(BF16)

    pltpu.make_async_copy(gbuf, gbuf, back_recv).wait()

    col = lax.broadcasted_iota(jnp.int32, (PAD_VARS, LONS), 1)

    def shifts(slot, v):
        stack[slot, 0] = jnp.where(col == 0, 0.0, pltpu.roll(v, 1, 1)).astype(BF16)
        stack[slot, 2] = jnp.where(col == LONS - 1, 0.0, pltpu.roll(v, LONS - 1, 1)).astype(BF16)

    gf[...] = gbuf[...].astype(F32)
    halo = []
    for r in range(2):
        v = jnp.concatenate([gf[pl.ds(2 * l + r, VARS, stride=8), :] for l in range(4)], axis=1)
        v = jnp.concatenate([v, jnp.zeros((PAD_VARS - VARS, LONS), F32)], axis=0)
        stack[r + 1, 1] = v.astype(BF16)
        halo.append(pltpu.make_async_remote_copy(
            src_ref=stack.at[r + 1, 1], dst_ref=stack.at[3 - 3 * r, 1],
            send_sem=halo_send.at[r], recv_sem=halo_recv.at[r],
            device_id=(ens, down if r == 0 else up, dp), device_id_type=MESH,
        ))
        halo[r].start()
        shifts(r + 1, v)

    to_core = []
    for a in (0, -1, 1):
        if a:
            rows_out[0 if a > 0 else 1].wait_recv()

            @pl.when(lat == (0 if a < 0 else BANDS - 1))
            def _(a=a):
                fs[0 if a < 0 else 3] = jnp.zeros((CHANS, LONS), BF16)

        acc = None
        for r in range(2):
            part = lax.dot_general(
                stack[r + 1].reshape(3 * PAD_VARS, LONS), fs[r + 1 + a],
                (((1,), (1,)), ((), ())), preferred_element_type=F32,
            )
            acc = part if acc is None else acc + part
        for b in range(3):
            for h in range(2):
                wg[h, a + 1, (2 - b) * VARS:(3 - b) * VARS, :] = acc[
                    b * PAD_VARS:b * PAD_VARS + VARS, h * 128:(h + 1) * 128
                ]
        copy = pltpu.make_async_remote_copy(
            src_ref=wg.at[1 - core, a + 1], dst_ref=wgin.at[a + 1],
            send_sem=core_send.at[a + 1], recv_sem=core_recv.at[a + 1],
            device_id=(other_core, lat, dp), device_id_type=MESH,
        )
        copy.start()
        to_core.append(copy)
    pl.semaphore_wait(pair_in, 1)
    for copy in to_core:
        copy.wait_recv()
    mine_sum = (wg[core] + wgin[...]).reshape(TAP_ROWS, 128)
    fill = jnp.zeros((PIECES * PIECE - TAP_ROWS, 128), F32)
    pieces[...] = jnp.concatenate([mine_sum, fill], axis=0).astype(BF16)

    def piece_of(chip, par):
        first = mod(mod(chip, 4) + div(chip, 4), 2) == par
        second = jnp.logical_and(chip == 3 * third(chip), chip < 15)
        return jnp.logical_or(first, second), jnp.where(first, chip, 16 + third(chip))

    spots = []
    for dz in (1, 0):
        for dx, dy in STEPS:
            if dx == dy == dz == 0:
                continue
            qx = mod(x + dx, 4)
            qy = mod(y + dy, 4)
            par = parity if dz == 0 else 1 - parity
            device = (mod(qy, 2) * 8 + qx * 2 + core, lat if dz == 0 else pair, div(qy, 2))
            spots.append((qy * 4 + qx, par, device))
    place = (y * 4 + x) * 2 + parity
    sums, piece = piece_of(y * 4 + x, parity)
    piece = jnp.where(sums, piece, 0)
    for chip, par, device in spots:
        theirs, q = piece_of(chip, par)

        @pl.when(theirs)
        def _(q=q, device=device):
            pltpu.make_async_remote_copy(
                src_ref=pieces.at[pl.ds(q * PIECE, PIECE)], dst_ref=rs.at[place],
                send_sem=rs_send, recv_sem=rs_recv, device_id=device, device_id_type=MESH,
            ).start()

    @pl.when(sums)
    def _():
        pltpu.make_async_copy(pieces.at[pl.ds(piece * PIECE, PIECE)], rs.at[place], rs_recv).start()

    for r in range(2):
        halo[r].wait_recv()
    for slot, edge in ((3, BANDS - 1), (0, 0)):
        v = jnp.where(lat == edge, 0.0, stack[slot, 1].astype(F32))
        stack[slot, 1] = v.astype(BF16)
        shifts(slot, v)
    for r in range(2):
        grad = lax.dot_general(
            weight[...], stack[pl.ds(r, 3)].reshape(9 * PAD_VARS, LONS),
            (((0,), (0,)), ((), ())), preferred_element_type=F32,
        )
        for l in range(4):
            ff[pl.ds(2 * l + r, CHANS, stride=8), :] = grad[:, l * 128:(l + 1) * 128]
    fg_ref[...] = ff[...].astype(BF16)

    pl.semaphore_wait(four_in, 2)

    @pl.when(sums)
    def _():
        pltpu.make_async_copy(rs, rs, rs_recv).wait()
        acc = rs[0].astype(F32)
        for q in range(1, 32):
            acc = acc + rs[q].astype(F32)
        zb[div(lat, 2)] = acc.astype(BF16)
        for to in range(8):

            @pl.when(div(lat, 2) != to)
            def _(to=to):
                pltpu.make_async_remote_copy(
                    src_ref=zb.at[div(lat, 2)], dst_ref=zb.at[div(lat, 2)], send_sem=zb_send, recv_sem=zb_recv,
                    device_id=(ens, 2 * to + parity, dp), device_id_type=MESH,
                ).start()

        pltpu.make_async_copy(zb.at[pl.ds(0, 7)], zb.at[pl.ds(0, 7)], zb_recv).wait()
        acc = zb[0].astype(F32)
        for q in range(1, 8):
            acc = acc + zb[q].astype(F32)
        total[...] = acc.astype(BF16)
        for l in range(2):
            for q in range(16):
                band_to = lat - parity + l

                @pl.when(jnp.logical_or(q != y * 4 + x, band_to != lat))
                def _(q=q, band_to=band_to):
                    pltpu.make_async_remote_copy(
                        src_ref=total, dst_ref=gw_ref.at[core, piece],
                        send_sem=ag_send, recv_sem=ag_recv,
                        device_id=(q % 8 * 2 + core, band_to, q // 8), device_id_type=MESH,
                    ).start()

        pltpu.make_async_copy(total, gw_ref.at[core, piece], ag_recv).start()

    pltpu.make_async_copy(gw_ref.at[core], gw_ref.at[core], ag_recv).wait()
    forward = pltpu.make_async_remote_copy(
        src_ref=gw_ref.at[core], dst_ref=gw_ref.at[core], send_sem=fwd_send, recv_sem=fwd_recv,
        device_id=(other_core, lat, dp), device_id_type=MESH,
    )
    forward.start()

    @pl.when(owned)
    def _():
        pltpu.make_async_copy(mbuf.at[pl.ds(0, OWNERS - 1)], mbuf.at[pl.ds(0, OWNERS - 1)], exch_send).wait()
        pltpu.make_async_copy(obuf.at[pl.ds(0, MEMBERS - 1)], obuf.at[pl.ds(0, MEMBERS - 1)], back_send).wait()

    @pl.when(jnp.logical_not(owned))
    def _():
        pltpu.make_async_copy(mbuf.at[pl.ds(0, OWNERS)], mbuf.at[pl.ds(0, OWNERS)], exch_send).wait()

    for r in range(2):
        rows_out[r].wait_send()
        halo[r].wait_send()
    for copy in to_core:
        copy.wait_send()

    @pl.when(sums)
    def _():
        pltpu.make_async_copy(rs.at[pl.ds(0, PIECES - 1)], rs.at[pl.ds(0, PIECES - 1)], rs_send).wait()
        pltpu.make_async_copy(zb.at[pl.ds(0, 7)], zb.at[pl.ds(0, 7)], zb_send).wait()
        pltpu.make_async_copy(rs.at[pl.ds(0, 31)], rs.at[pl.ds(0, 31)], ag_send).wait()

    @pl.when(jnp.logical_not(sums))
    def _():
        pltpu.make_async_copy(rs.at[pl.ds(0, PIECES)], rs.at[pl.ds(0, PIECES)], rs_send).wait()

    forward.wait()


def write_results(factor, fg_ref, gw_ref, fg_out, gw_out, outbuf, sems):
    copies = [pltpu.make_async_copy(fg_ref, fg_out, sems.at[3])]
    copies[0].start()
    for i in range(3):
        rows = pl.ds(i * 3 * VARS, 3 * VARS)
        for c in range(2):
            wide = gw_ref[c].reshape(PIECES * PIECE, 128).astype(F32)
            outbuf[rows, c * 128:(c + 1) * 128] = wide[i * 3 * VARS:(i + 1) * 3 * VARS] * factor
        copies.append(pltpu.make_async_copy(outbuf.at[rows], gw_out.at[rows], sems.at[i]))
        copies[-1].start()
    for copy in copies:
        copy.wait()


def raw_rows(v):
    lead = v.shape[0]
    return v.reshape(lead, 2, 4, 128).transpose(0, 2, 1, 3).reshape(lead * 8, 128)


def local(features, members_out, observed, conv_weight, lat_weight, var_weight, land_mask):
    hbm = pl.BlockSpec(memory_space=pltpu.HBM)
    vmem = pl.BlockSpec(memory_space=pltpu.VMEM)
    dma = pltpu.SemaphoreType.DMA
    regular = pltpu.SemaphoreType.REGULAR
    fg, gw = pl.pallas_call(
        kernel,
        out_shape=(
            pltpu.VMEM((CHANS * 8, 128), BF16),
            pltpu.VMEM((2, PIECES, PIECE, 128), BF16),
        ),
        in_specs=[hbm] * 7,
        out_specs=(vmem, vmem),
        scratch_shapes=[
            pltpu.VMEM((RAW, 128), BF16),
            pltpu.VMEM((MEMBERS, CHUNK, 128), BF16),
            pltpu.VMEM((MEMBERS, CHUNK, 128), BF16),
            pltpu.VMEM((RAW, 128), BF16),
            pltpu.VMEM((RAW, 128), F32),
            pltpu.VMEM((CHUNK, 128), F32),
            pltpu.SMEM((2,), F32),
            pltpu.SMEM((VARS,), F32),
            pltpu.VMEM((8, 128), jnp.int32),
            pltpu.VMEM((CHANS * 8, 128), BF16),
            pltpu.VMEM((CHANS * 8, 128), F32),
            pltpu.VMEM((4, CHANS, LONS), BF16),
            pltpu.VMEM((9, VARS, CHANS), BF16),
            pltpu.VMEM((9 * PAD_VARS, CHANS), BF16),
            pltpu.VMEM((4, 3, PAD_VARS, LONS), BF16),
            pltpu.VMEM((2, 3, 3 * VARS, 128), F32),
            pltpu.VMEM((3, 3 * VARS, 128), F32),
            pltpu.VMEM((PIECES * PIECE, 128), BF16),
            pltpu.VMEM((32, PIECE, 128), BF16),
            pltpu.VMEM((8, PIECE, 128), BF16),
            pltpu.VMEM((PIECE, 128), BF16),
            dma, dma, dma, dma, dma((2,)), dma((2,)), dma((2,)), dma((2,)), dma((3,)), dma((3,)),
            dma, dma, dma, dma, dma, dma, dma, dma, dma((7,)),
            regular, regular, regular, regular, regular,
        ],
        compiler_params=pltpu.CompilerParams(
            collective_id=0, has_side_effects=True, vmem_limit_bytes=48 * 1024 * 1024
        ),
        name="crps_backward",
    )(*(
        pltpu.with_memory_space_constraint(v, pltpu.HBM)
        for v in (
            raw_rows(members_out[0, 0]), raw_rows(observed[0]), raw_rows(features[0, 0]), conv_weight,
            lat_weight, var_weight, raw_rows(land_mask[None]),
        )
    ))
    factor = 1.0 / math.sqrt(2 * MEMBERS * 32 * LONS)

    def body(*refs):
        write_results(factor, *refs)

    feature_grad, grad_weight = pl.pallas_call(
        body,
        out_shape=(
            jax.ShapeDtypeStruct((CHANS * 8, 128), BF16),
            jax.ShapeDtypeStruct((TAP_ROWS, CHANS), F32),
        ),
        in_specs=[vmem, vmem],
        out_specs=(hbm, hbm),
        scratch_shapes=[
            pltpu.VMEM((TAP_ROWS, CHANS), F32),
            dma((4,)),
        ],
        compiler_params=pltpu.CompilerParams(vmem_limit_bytes=48 * 1024 * 1024),
        name="write_results",
    )(*(pltpu.with_memory_space_constraint(v, pltpu.VMEM) for v in (fg, gw)))
    feature_grad = feature_grad.reshape(CHANS, 4, 2, 128).transpose(0, 2, 1, 3).reshape(1, 1, CHANS, 2, LONS)
    return (feature_grad, grad_weight.reshape(9, VARS, CHANS))


def solution(mesh):
    return jax.shard_map(
        local,
        mesh=mesh,
        in_specs=(
            P("dp", "ens", None, "lat", None),
            P("dp", "ens", None, "lat", None),
            P("dp", None, "lat", None),
            P(),
            P("lat"),
            P(),
            P("lat", None),
        ),
        out_specs=(P("dp", "ens", None, "lat", None), P()),
        check_vma=False,
    )
```

```python
import math

import jax
import jax.numpy as jnp
from jax import lax
from jax.experimental import pallas as pl
from jax.experimental.pallas import tpu as pltpu
from jax.sharding import PartitionSpec as P

MESH = pl.DeviceIdType.MESH
BF16 = jnp.bfloat16
F32 = jnp.float32

MEMBERS = 16
BANDS = 16
VARS = 72
PAD_VARS = 80
LONS = 512
CHANS = 256
OWNERS = 12
CHUNK = 48
RAW = VARS * 8
TAP_ROWS = 9 * VARS
PIECES = 21
PIECE = 32
STEPS = sorted(
    ((dx, dy) for dx in range(4) for dy in range(4)),
    key=lambda s: -(min(s[0], 4 - s[0]) + min(s[1], 4 - s[1])),
)


def div(v, n):
    return lax.shift_right_logical(v, n.bit_length() - 1)


def mod(v, n):
    return lax.bitwise_and(v, n - 1)


def third(v):
    return lax.shift_right_logical(v * 11, 5)


def kernel(
    members_ref, obs_ref, feats_ref, weight_ref, lat_ref, var_ref, land_ref,
    fg_ref, gw_ref,
    members, mbuf, obuf, gbuf, gf, obs, lats, vars_, land, fraw, ff, fs, wraw, weight, stack, wg, wgin, pieces, rs, zb, total,
    exch_send, exch_recv, back_send, back_recv, feat_send, feat_recv, halo_send, halo_recv, core_send, core_recv,
    rs_send, rs_recv, zb_send, zb_recv, ag_send, ag_recv, fwd_send, fwd_recv, load_sem,
    dp_in, pair_in, one_in, two_in, four_in,
):
    ens = lax.axis_index("ens")
    lat = lax.axis_index("lat")
    dp = lax.axis_index("dp")
    core = mod(ens, 2)
    x = div(mod(ens, 8), 2)
    ylo = div(ens, 8)
    y = dp * 2 + ylo
    up = mod(lat + 1, BANDS)
    down = mod(lat + BANDS - 1, BANDS)
    parity = mod(lat, 2)
    pair = lat + 1 - 2 * parity
    other_core = ens + 1 - 2 * core

    def band(step):
        return mod(lat + step, BANDS)

    def tell(sem, device):
        pl.semaphore_signal(sem, inc=1, device_id=device, device_id_type=MESH)

    barrier = pltpu.get_barrier_semaphore()

    for dx, dy in STEPS:
        for dc in range(2):
            if dy <= 1 and (dx or dy or dc):
                tell(barrier, (mod(ylo + dy, 2) * 8 + mod(x + dx, 4) * 2 + mod(core + dc, 2), lat, dp))
    tell(barrier, (ens, up, dp))
    tell(barrier, (ens, down, dp))
    tell(barrier, (ens, lat, 1 - dp))

    def chunk_of(e):
        pos = mod(e, 4)
        first = jnp.where(e < 8, 1, 3)
        owns = pos != first
        return owns, div(e, 4) * 3 + pos - jnp.where(pos > first, 1, 0)

    owned, mine = chunk_of(ens)
    mine = jnp.where(owned, mine, 0)

    loads = [
        pltpu.make_async_copy(src, dst, load_sem.at[i])
        for i, (src, dst) in enumerate((
            (members_ref, members),
            (feats_ref, fraw),
            (obs_ref.at[pl.ds(mine * CHUNK, CHUNK)], obs),
            (weight_ref, wraw),
            (land_ref, land),
            (lat_ref, lats),
            (var_ref, vars_),
        ))
    ]
    for load in loads:
        load.start()
    loads[0].wait()

    pl.semaphore_wait(barrier, 15 + 3)

    for kind in range(4):

        @pl.when(core * 2 + mod(x + ylo, 2) == kind)
        def _(kind=kind):
            for dx, dy in STEPS:
                for dc in range(2):
                    if dy > 1 or dx == dy == dc == 0:
                        continue
                    if (kind // 2 + dc) % 2 == 1 and (kind + dx + dy) % 2 == 0:
                        continue
                    to = mod(ylo + dy, 2) * 8 + mod(x + dx, 4) * 2 + (kind // 2 + dc) % 2
                    pltpu.make_async_remote_copy(
                        src_ref=members.at[pl.ds(chunk_of(to)[1] * CHUNK, CHUNK)], dst_ref=mbuf.at[ens],
                        send_sem=exch_send, recv_sem=exch_recv,
                        device_id=(to, lat, dp), device_id_type=MESH,
                    ).start()

    @pl.when(owned)
    def _():
        pltpu.make_async_copy(members.at[pl.ds(mine * CHUNK, CHUNK)], mbuf.at[ens], exch_recv).start()

    tell(dp_in, (ens, lat, 1 - dp))
    tell(one_in, (ens, up, dp))
    tell(one_in, (ens, down, dp))

    loads[1].wait()
    ff[...] = fraw[...].astype(F32)
    rows_out = []
    for r in range(2):
        for l in range(4):
            fs[r + 1, :, l * 128:(l + 1) * 128] = ff[pl.ds(2 * l + r, CHANS, stride=8), :].astype(BF16)
        rows_out.append(pltpu.make_async_remote_copy(
            src_ref=fs.at[r + 1], dst_ref=fs.at[3 - 3 * r],
            send_sem=feat_send.at[r], recv_sem=feat_recv.at[r],
            device_id=(ens, down if r == 0 else up, dp), device_id_type=MESH,
        ))
        rows_out[r].start()
    for load in loads[2:]:
        load.wait()
    pl.semaphore_wait(one_in, 2)
    tell(two_in, (ens, band(2), dp))
    tell(two_in, (ens, band(BANDS - 2), dp))

    @pl.when(owned)
    def _():
        pltpu.make_async_copy(mbuf, mbuf, exch_recv).wait()

        one = jnp.ones((16, 128), F32)
        zero = jnp.zeros((16, 128), F32)
        row = lax.broadcasted_iota(jnp.int32, (8, 128), 0)
        lat_rows = jnp.where(lax.rem(row, 2) == 0, lats[0], lats[1])
        land_rows = 1.0 + land[...].astype(F32)

        def tile(u, c):
            rows = pl.ds(pl.multiple_of(u * 16, 16), 16)
            vals = [mbuf[m, rows, :].astype(F32) for m in range(MEMBERS)]
            sums = [None] * MEMBERS
            for i in range(MEMBERS):
                for j in range(i + 1, MEMBERS):
                    s = jnp.where(vals[i] > vals[j], one, jnp.where(vals[i] < vals[j], -one, zero))
                    sums[i] = s if sums[i] is None else sums[i] + s
                    sums[j] = -s if sums[j] is None else sums[j] - s
            seen = obs[rows, :]
            v0 = mine * 6 + u * 2
            cell = jnp.concatenate(
                [(lat_rows * vars_[v0]) * land_rows, (lat_rows * vars_[v0 + 1]) * land_rows], axis=0
            )
            for m in range(MEMBERS):
                s = jnp.where(vals[m] > seen, one, jnp.where(vals[m] < seen, -one, zero))
                obuf[m, rows, :] = (cell * (s - sums[m] / (MEMBERS - 1))).astype(BF16)
            return c

        lax.fori_loop(0, CHUNK // 16, tile, 0)

        for dx, dy in STEPS:
            if dy > 1:
                continue
            for dc in range(2):
                if dx == dy == dc == 0:
                    continue
                to = mod(ylo + dy, 2) * 8 + mod(x + dx, 4) * 2 + mod(core + dc, 2)
                pltpu.make_async_remote_copy(
                    src_ref=obuf.at[to], dst_ref=gbuf.at[pl.ds(mine * CHUNK, CHUNK)],
                    send_sem=back_send, recv_sem=back_recv,
                    device_id=(to, lat, dp), device_id_type=MESH,
                ).start()
        pltpu.make_async_copy(obuf.at[ens], gbuf.at[pl.ds(mine * CHUNK, CHUNK)], back_recv).start()

    pl.semaphore_wait(dp_in, 1)
    tell(pair_in, (ens, pair, dp))
    pl.semaphore_wait(two_in, 2)
    tell(four_in, (ens, band(4), dp))
    tell(four_in, (ens, band(BANDS - 4), dp))

    for t in range(9):
        taps = jnp.concatenate(
            [wraw[8 - t].astype(F32), jnp.zeros((PAD_VARS - VARS, CHANS), F32)], axis=0
        )
        weight[t * PAD_VARS:(t + 1) * PAD_VARS, :] = taps.astype(BF16)

    pltpu.make_async_copy(gbuf, gbuf, back_recv).wait()

    col = lax.broadcasted_iota(jnp.int32, (PAD_VARS, LONS), 1)

    def shifts(slot, v):
        stack[slot, 0] = jnp.where(col == 0, 0.0, pltpu.roll(v, 1, 1)).astype(BF16)
        stack[slot, 2] = jnp.where(col == LONS - 1, 0.0, pltpu.roll(v, LONS - 1, 1)).astype(BF16)

    gf[...] = gbuf[...].astype(F32)
    halo = []
    for r in range(2):
        v = jnp.concatenate([gf[pl.ds(2 * l + r, VARS, stride=8), :] for l in range(4)], axis=1)
        v = jnp.concatenate([v, jnp.zeros((PAD_VARS - VARS, LONS), F32)], axis=0)
        stack[r + 1, 1] = v.astype(BF16)
        halo.append(pltpu.make_async_remote_copy(
            src_ref=stack.at[r + 1, 1], dst_ref=stack.at[3 - 3 * r, 1],
            send_sem=halo_send.at[r], recv_sem=halo_recv.at[r],
            device_id=(ens, down if r == 0 else up, dp), device_id_type=MESH,
        ))
        halo[r].start()
        shifts(r + 1, v)

    to_core = []
    for a in (0, -1, 1):
        if a:
            rows_out[0 if a > 0 else 1].wait_recv()

            @pl.when(lat == (0 if a < 0 else BANDS - 1))
            def _(a=a):
                fs[0 if a < 0 else 3] = jnp.zeros((CHANS, LONS), BF16)

        acc = None
        for r in range(2):
            part = lax.dot_general(
                stack[r + 1].reshape(3 * PAD_VARS, LONS), fs[r + 1 + a],
                (((1,), (1,)), ((), ())), preferred_element_type=F32,
            )
            acc = part if acc is None else acc + part
        for b in range(3):
            for h in range(2):
                wg[h, a + 1, (2 - b) * VARS:(3 - b) * VARS, :] = acc[
                    b * PAD_VARS:b * PAD_VARS + VARS, h * 128:(h + 1) * 128
                ]
        copy = pltpu.make_async_remote_copy(
            src_ref=wg.at[1 - core, a + 1], dst_ref=wgin.at[a + 1],
            send_sem=core_send.at[a + 1], recv_sem=core_recv.at[a + 1],
            device_id=(other_core, lat, dp), device_id_type=MESH,
        )
        copy.start()
        to_core.append(copy)
    pl.semaphore_wait(pair_in, 1)
    for copy in to_core:
        copy.wait_recv()
    mine_sum = (wg[core] + wgin[...]).reshape(TAP_ROWS, 128)
    fill = jnp.zeros((PIECES * PIECE - TAP_ROWS, 128), F32)
    pieces[...] = jnp.concatenate([mine_sum, fill], axis=0).astype(BF16)

    def piece_of(chip, par):
        first = mod(mod(chip, 4) + div(chip, 4), 2) == par
        second = jnp.logical_and(chip == 3 * third(chip), chip < 15)
        return jnp.logical_or(first, second), jnp.where(first, chip, 16 + third(chip))

    spots, order = [], []
    for dz in (1, 0):
        for dx, dy in STEPS:
            if dx == dy == dz == 0:
                continue
            qx = mod(x + dx, 4)
            qy = mod(y + dy, 4)
            par = parity if dz == 0 else 1 - parity
            device = (mod(qy, 2) * 8 + qx * 2 + core, lat if dz == 0 else pair, div(qy, 2))
            order.append((dx, dy, dz))
            spots.append((qy * 4 + qx, par, device))
    place = (y * 4 + x) * 2 + parity
    sums, piece = piece_of(y * 4 + x, parity)
    piece = jnp.where(sums, piece, 0)
    self_first = mod(x + y + parity, 2) == 0

    def send_piece(q, device):
        pltpu.make_async_remote_copy(
            src_ref=pieces.at[pl.ds(q * PIECE, PIECE)], dst_ref=rs.at[place],
            send_sem=rs_send, recv_sem=rs_recv, device_id=device, device_id_type=MESH,
        ).start()

    for odd, case in ((0, self_first), (1, jnp.logical_not(self_first))):

        @pl.when(case)
        def _(odd=odd):
            for (chip, par, device), (dx, dy, dz) in zip(spots, order):
                if (dx + dy + dz) % 2 == odd:
                    send_piece(chip, device)
                else:
                    q = third(chip)

                    @pl.when(jnp.logical_and(chip == 3 * q, chip < 15))
                    def _(q=q, device=device):
                        send_piece(16 + q, device)

    @pl.when(sums)
    def _():
        pltpu.make_async_copy(pieces.at[pl.ds(piece * PIECE, PIECE)], rs.at[place], rs_recv).start()

    for r in range(2):
        halo[r].wait_recv()
    for slot, edge in ((3, BANDS - 1), (0, 0)):
        v = jnp.where(lat == edge, 0.0, stack[slot, 1].astype(F32))
        stack[slot, 1] = v.astype(BF16)
        shifts(slot, v)
    for r in range(2):
        grad = lax.dot_general(
            weight[...], stack[pl.ds(r, 3)].reshape(9 * PAD_VARS, LONS),
            (((0,), (0,)), ((), ())), preferred_element_type=F32,
        )
        for l in range(4):
            ff[pl.ds(2 * l + r, CHANS, stride=8), :] = grad[:, l * 128:(l + 1) * 128]
    fg_ref[...] = ff[...].astype(BF16)

    pl.semaphore_wait(four_in, 2)

    @pl.when(sums)
    def _():
        pltpu.make_async_copy(rs, rs, rs_recv).wait()
        acc = rs[0].astype(F32)
        for q in range(1, 32):
            acc = acc + rs[q].astype(F32)
        zb[div(lat, 2)] = acc.astype(BF16)
        for to in range(8):

            @pl.when(div(lat, 2) != to)
            def _(to=to):
                pltpu.make_async_remote_copy(
                    src_ref=zb.at[div(lat, 2)], dst_ref=zb.at[div(lat, 2)], send_sem=zb_send, recv_sem=zb_recv,
                    device_id=(ens, 2 * to + parity, dp), device_id_type=MESH,
                ).start()

        pltpu.make_async_copy(zb.at[pl.ds(0, 7)], zb.at[pl.ds(0, 7)], zb_recv).wait()
        acc = zb[0].astype(F32)
        for q in range(1, 8):
            acc = acc + zb[q].astype(F32)
        total[...] = acc.astype(BF16)
        for l in range(2):
            for q in range(16):
                band_to = lat - parity + l

                @pl.when(jnp.logical_or(q != y * 4 + x, band_to != lat))
                def _(q=q, band_to=band_to):
                    pltpu.make_async_remote_copy(
                        src_ref=total, dst_ref=gw_ref.at[core, piece],
                        send_sem=ag_send, recv_sem=ag_recv,
                        device_id=(q % 8 * 2 + core, band_to, q // 8), device_id_type=MESH,
                    ).start()

        pltpu.make_async_copy(total, gw_ref.at[core, piece], ag_recv).start()

    pltpu.make_async_copy(gw_ref.at[core], gw_ref.at[core], ag_recv).wait()
    forward = pltpu.make_async_remote_copy(
        src_ref=gw_ref.at[core], dst_ref=gw_ref.at[core], send_sem=fwd_send, recv_sem=fwd_recv,
        device_id=(other_core, lat, dp), device_id_type=MESH,
    )
    forward.start()

    @pl.when(owned)
    def _():
        pltpu.make_async_copy(mbuf.at[pl.ds(0, OWNERS - 1)], mbuf.at[pl.ds(0, OWNERS - 1)], exch_send).wait()
        pltpu.make_async_copy(obuf.at[pl.ds(0, MEMBERS - 1)], obuf.at[pl.ds(0, MEMBERS - 1)], back_send).wait()

    @pl.when(jnp.logical_not(owned))
    def _():
        pltpu.make_async_copy(mbuf.at[pl.ds(0, OWNERS)], mbuf.at[pl.ds(0, OWNERS)], exch_send).wait()

    for r in range(2):
        rows_out[r].wait_send()
        halo[r].wait_send()
    for copy in to_core:
        copy.wait_send()

    @pl.when(sums)
    def _():
        pltpu.make_async_copy(rs.at[pl.ds(0, PIECES - 1)], rs.at[pl.ds(0, PIECES - 1)], rs_send).wait()
        pltpu.make_async_copy(zb.at[pl.ds(0, 7)], zb.at[pl.ds(0, 7)], zb_send).wait()
        pltpu.make_async_copy(rs.at[pl.ds(0, 31)], rs.at[pl.ds(0, 31)], ag_send).wait()

    @pl.when(jnp.logical_not(sums))
    def _():
        pltpu.make_async_copy(rs.at[pl.ds(0, PIECES)], rs.at[pl.ds(0, PIECES)], rs_send).wait()

    forward.wait()


def write_results(factor, fg_ref, gw_ref, fg_out, gw_out, outbuf, sems):
    copies = [pltpu.make_async_copy(fg_ref, fg_out, sems.at[3])]
    copies[0].start()
    for i in range(3):
        rows = pl.ds(i * 3 * VARS, 3 * VARS)
        for c in range(2):
            wide = gw_ref[c].reshape(PIECES * PIECE, 128).astype(F32)
            outbuf[rows, c * 128:(c + 1) * 128] = wide[i * 3 * VARS:(i + 1) * 3 * VARS] * factor
        copies.append(pltpu.make_async_copy(outbuf.at[rows], gw_out.at[rows], sems.at[i]))
        copies[-1].start()
    for copy in copies:
        copy.wait()


def raw_rows(v):
    lead = v.shape[0]
    return v.reshape(lead, 2, 4, 128).transpose(0, 2, 1, 3).reshape(lead * 8, 128)


def local(features, members_out, observed, conv_weight, lat_weight, var_weight, land_mask):
    hbm = pl.BlockSpec(memory_space=pltpu.HBM)
    vmem = pl.BlockSpec(memory_space=pltpu.VMEM)
    dma = pltpu.SemaphoreType.DMA
    regular = pltpu.SemaphoreType.REGULAR
    fg, gw = pl.pallas_call(
        kernel,
        out_shape=(
            pltpu.VMEM((CHANS * 8, 128), BF16),
            pltpu.VMEM((2, PIECES, PIECE, 128), BF16),
        ),
        in_specs=[hbm] * 7,
        out_specs=(vmem, vmem),
        scratch_shapes=[
            pltpu.VMEM((RAW, 128), BF16),
            pltpu.VMEM((MEMBERS, CHUNK, 128), BF16),
            pltpu.VMEM((MEMBERS, CHUNK, 128), BF16),
            pltpu.VMEM((RAW, 128), BF16),
            pltpu.VMEM((RAW, 128), F32),
            pltpu.VMEM((CHUNK, 128), F32),
            pltpu.SMEM((2,), F32),
            pltpu.SMEM((VARS,), F32),
            pltpu.VMEM((8, 128), jnp.int32),
            pltpu.VMEM((CHANS * 8, 128), BF16),
            pltpu.VMEM((CHANS * 8, 128), F32),
            pltpu.VMEM((4, CHANS, LONS), BF16),
            pltpu.VMEM((9, VARS, CHANS), BF16),
            pltpu.VMEM((9 * PAD_VARS, CHANS), BF16),
            pltpu.VMEM((4, 3, PAD_VARS, LONS), BF16),
            pltpu.VMEM((2, 3, 3 * VARS, 128), F32),
            pltpu.VMEM((3, 3 * VARS, 128), F32),
            pltpu.VMEM((PIECES * PIECE, 128), BF16),
            pltpu.VMEM((32, PIECE, 128), BF16),
            pltpu.VMEM((8, PIECE, 128), BF16),
            pltpu.VMEM((PIECE, 128), BF16),
            dma, dma, dma, dma, dma((2,)), dma((2,)), dma((2,)), dma((2,)), dma((3,)), dma((3,)),
            dma, dma, dma, dma, dma, dma, dma, dma, dma((7,)),
            regular, regular, regular, regular, regular,
        ],
        compiler_params=pltpu.CompilerParams(
            collective_id=0, has_side_effects=True, vmem_limit_bytes=48 * 1024 * 1024
        ),
        name="crps_backward",
    )(*(
        pltpu.with_memory_space_constraint(v, pltpu.HBM)
        for v in (
            raw_rows(members_out[0, 0]), raw_rows(observed[0]), raw_rows(features[0, 0]), conv_weight,
            lat_weight, var_weight, raw_rows(land_mask[None]),
        )
    ))
    factor = 1.0 / math.sqrt(2 * MEMBERS * 32 * LONS)

    def body(*refs):
        write_results(factor, *refs)

    feature_grad, grad_weight = pl.pallas_call(
        body,
        out_shape=(
            jax.ShapeDtypeStruct((CHANS * 8, 128), BF16),
            jax.ShapeDtypeStruct((TAP_ROWS, CHANS), F32),
        ),
        in_specs=[vmem, vmem],
        out_specs=(hbm, hbm),
        scratch_shapes=[
            pltpu.VMEM((TAP_ROWS, CHANS), F32),
            dma((4,)),
        ],
        compiler_params=pltpu.CompilerParams(vmem_limit_bytes=48 * 1024 * 1024),
        name="write_results",
    )(*(pltpu.with_memory_space_constraint(v, pltpu.VMEM) for v in (fg, gw)))
    feature_grad = feature_grad.reshape(CHANS, 4, 2, 128).transpose(0, 2, 1, 3).reshape(1, 1, CHANS, 2, LONS)
    return (feature_grad, grad_weight.reshape(9, VARS, CHANS))


def solution(mesh):
    return jax.shard_map(
        local,
        mesh=mesh,
        in_specs=(
            P("dp", "ens", None, "lat", None),
            P("dp", "ens", None, "lat", None),
            P("dp", None, "lat", None),
            P(),
            P("lat"),
            P(),
            P("lat", None),
        ),
        out_specs=(P("dp", "ens", None, "lat", None), P()),
        check_vma=False,
    )
```
